256 devices in a mesh: head: 8 (over y, core), ctx: 32 (over z, x).
Axes of the slice: x: 4, y: 4, z: 8, core: 2. Of those that a mesh axis runs over, the one named last changes fastest.
Arguments:
- queries: bfloat16 [65536, 4096], P('ctx', 'head'), may hold values from -6 to 6
- keys: bfloat16 [65536, 4096], P('ctx', 'head'), may hold values from -6 to 6
- values: bfloat16 [65536, 4096], P('ctx', 'head'), may hold values from -23 to 23
- level_table: float32 [4, 9], replicated, may hold values from 0.3 to 3
- head_table: int32 [32], replicated, may hold values from 0 to 3
- gain: float32 [4096], P('head'), may hold values from 0.5 to 1.5
Outputs:
- attended: bfloat16 [65536, 4096], P('ctx', 'head')
The draws below stay inside these ranges and needn't reach their ends.
All inputs are finite; a program needn't handle non-finite values.
Results may differ from the reference program's by a relative error of at most 0.0043.
Values sent between devices are 32-bit elements; how exact they have to be, the bound alone decides.
A program may use at most 192 MiB of HBM per device.

```python
import math
import jax
import jax.numpy as jnp
from jax import lax

HEADS = 32
HEAD_DIM = 128
LEAF = 256
PROFILES = 4
SEG = 2048
TOKENS = 65536
D = 4096
LOCAL_BITS = 3
CTX_BITS = 5
LEVELS = 9
N_CTX = 32


def draw_values(key, part):
    first_key, second_key = jax.random.split(key, 2)
    head_ramp = jnp.arange(HEADS, dtype=jnp.float32) / max(HEADS - 1, 1)
    head_scale = jnp.exp(jnp.log(3.0) * head_ramp) * jax.random.uniform(second_key, (HEADS,), jnp.float32, 0.8, 1.25)
    columns = jnp.repeat(head_scale, HEAD_DIM)
    base = jnp.clip(jax.random.normal(first_key, (TOKENS, D), jnp.float32), -6.0, 6.0)
    return (base * columns[None, :]).astype(jnp.bfloat16)


def with_ends(array, rng, low, top_value):
    longest = array.shape.index(max(array.shape))
    spots = []
    for shift in (0, 1):
        where = [jax.random.randint(jax.random.fold_in(rng, axis), (), 0, length) for axis, length in enumerate(array.shape)]
        where[longest] = (where[longest] + shift) % array.shape[longest]
        spots.append(tuple(where))
    return array.at[spots[0]].set(low).at[spots[1]].set(top_value)


def level_of(stream_key, dims, cuts, low, top_value):
    level = 1.0
    for axis_at, blocks in cuts:
        draws = jax.random.uniform(jax.random.fold_in(jax.random.fold_in(stream_key, 6), axis_at), (blocks,), jnp.float32, low / len(cuts), top_value / len(cuts))
        level = level * jnp.repeat(jnp.exp(draws), dims[axis_at] // blocks).reshape((-1,) + (1,) * (len(dims) - 1 - axis_at))
    return level


def scatter_about(own_key, extent, scale, most, shards=(), kind=jnp.bfloat16):
    loudness = level_of(own_key, extent, shards, -0.22, 0.18) if shards else 1.0
    array = jax.random.normal(own_key, extent, jnp.float32) * scale * loudness
    return jnp.minimum(jnp.maximum(array, -most), most).astype(kind)


def setup_inputs(seed: int = 0) -> dict:
    arg_keys = jax.random.split(jax.random.key(seed), 7)
    queries = scatter_about(arg_keys[0], (TOKENS, D), 1.0, 6.0, ((0, 32), (1, 8)))
    keys = scatter_about(arg_keys[1], (TOKENS, D), 1.0, 6.0, ((0, 32), (1, 8)))
    values = draw_values(jax.random.fold_in(arg_keys[6], 71), 0)
    level_table = jnp.clip(jnp.exp(jax.random.uniform(arg_keys[3], (PROFILES, LEVELS), jnp.float32, math.log(0.3), math.log(3.0))), 0.3, 3.0)
    head_table = with_ends(jax.random.randint(arg_keys[4], (HEADS,), 0, PROFILES), jax.random.fold_in(arg_keys[4], 1), 0, PROFILES - 1).astype(jnp.int32)
    gain = jnp.clip(1.0 + 0.1 * jax.random.normal(arg_keys[5], (D,), jnp.float32), 0.5, 1.5)
    return dict(queries=queries, keys=keys, values=values, level_table=level_table, head_table=head_table, gain=gain)


epsilon = 1e-06

def level_scales(level_count):
    level_ids = jnp.arange(level_count, dtype=jnp.int32)
    bucket_sizes = jnp.exp2(jnp.maximum(level_ids - 1, 0).astype(jnp.float32)) * jnp.float32(LEAF)
    return 1.0 / jnp.sqrt(bucket_sizes)

def tile_levels(query_pos, key_pos, local_bits):
    distance = jnp.bitwise_xor((query_pos // LEAF)[:, None], (key_pos // LEAF)[None, :])
    level_ids = jnp.zeros(distance.shape, jnp.int32)
    for level_bit in range(local_bits):
        level_ids = level_ids + (distance >= 1 << level_bit).astype(jnp.int32)
    return level_ids

def tile_weights(query_pos, key_pos, effective, local_bits):
    level_ids = tile_levels(query_pos, key_pos, local_bits)
    weight = jnp.zeros((effective.shape[0],) + level_ids.shape, effective.dtype)
    for level_num in range(local_bits + 1):
        member = jnp.where(level_ids == level_num, 1.0, 0.0).astype(effective.dtype)
        weight = weight + member[None] * effective[:, level_num, None, None]
    causal = key_pos[None, :] <= query_pos[:, None]
    return jnp.where(causal[None], weight, 0.0)

def reference(queries, keys, values, level_table, head_table, gain):
    selector = (head_table[:, None] == jnp.arange(PROFILES, dtype=jnp.int32)[None, :]).astype(jnp.float32)
    chosen = jnp.dot(selector, level_table, precision=lax.Precision.HIGHEST)
    effective = chosen * level_scales(LEVELS)[None, :]
    query_all = queries.reshape(N_CTX, SEG, HEADS, HEAD_DIM)
    key_all = keys.reshape(N_CTX, SEG, HEADS, HEAD_DIM)
    value_all = values.reshape(N_CTX, SEG, HEADS, HEAD_DIM)

    def segment_state(operand):
        return jnp.einsum('thd,the->hde', operand[0].astype(jnp.float32), operand[1].astype(jnp.float32))
    states = lax.map(segment_state, (key_all, value_all))
    segment_ids = jnp.arange(N_CTX, dtype=jnp.int32)
    distant = jnp.zeros_like(states)
    for level_bit in range(CTX_BITS):
        grouped = states.reshape(N_CTX >> level_bit + 1, 2, 1 << level_bit, HEADS, HEAD_DIM, HEAD_DIM)
        sibling_sums = lax.optimization_barrier(jnp.sum(grouped[:, 0], axis=1))
        siblings = jnp.repeat(sibling_sums, 2 << level_bit, axis=0)
        member = (segment_ids >> level_bit & 1).astype(jnp.float32)
        factor = member[:, None] * effective[None, :, LOCAL_BITS + 1 + level_bit]
        distant = distant + factor[:, :, None, None] * siblings
    key_pos = jnp.arange(SEG, dtype=jnp.int32)

    def segment_out(operand):
        query_seg, key_seg, value_seg, distant_seg = operand

        def head_out(inner):
            query_head, key_head, value_head, eff_row = inner
            scores = jnp.dot(query_head, key_head.T, preferred_element_type=jnp.float32)
            weight = tile_weights(key_pos, key_pos, eff_row[None, :], LOCAL_BITS)[0]
            rounded = (scores * weight).astype(jnp.bfloat16)
            return jnp.dot(rounded, value_head, preferred_element_type=jnp.float32)
        nearby = lax.map(head_out, (jnp.swapaxes(query_seg, 0, 1), jnp.swapaxes(key_seg, 0, 1), jnp.swapaxes(value_seg, 0, 1), effective))
        nearby = jnp.swapaxes(nearby, 0, 1)
        remote = jnp.einsum('thd,hde->the', query_seg.astype(jnp.float32), distant_seg, precision=lax.Precision.HIGHEST)
        return nearby + remote
    combined = lax.map(segment_out, (query_all, key_all, value_all, distant)).reshape(TOKENS, D)
    squares = lax.optimization_barrier(jnp.sum(combined * combined, axis=1))
    inverse = lax.rsqrt(squares / D + epsilon)
    return (combined * inverse[:, None] * gain[None, :]).astype(jnp.bfloat16)
```

```python
import functools

import jax
import jax.numpy as jnp
import numpy as np
from jax import lax
from jax.experimental import pallas as pl
from jax.experimental.pallas import tpu as pltpu
from jax.sharding import PartitionSpec as P

HEAD_DIM = 128
LEAF = 256
LEAVES = 8
D = 4096
HEADS_HERE = 4
SEG = LEAF * LEAVES
WIDTH = HEADS_HERE * HEAD_DIM
NX, NZ, NH = 4, 8, 8
SLICE = HEAD_DIM // NZ
CHUNKS = 2
ROWS = SEG // CHUNKS
EPSILON = 1e-06
MESH = pl.DeviceIdType.MESH
SCALES = [float(np.float32(1.0) / np.sqrt(np.float32(LEAF * 2 ** max(l - 1, 0)))) for l in range(9)]

NT = (((1,), (1,)), ((), ()))
TN = (((0,), (0,)), ((), ()))


def dot(a, b, dims=(((1,), (0,)), ((), ()))):
    return lax.dot_general(a, b, dims, preferred_element_type=jnp.float32)


def fenwick(states, one, two, four=None):
    out = []
    pair = states[0] + states[1]
    out.append(None)
    out.append(one * states[0])
    out.append(two * pair)
    out.append(out[2] + one * states[2])
    if four is None:
        return out
    pair_b = states[4] + states[5]
    quad = four * (pair + (states[2] + states[3]))
    out.append(quad)
    out.append(quad + one * states[4])
    out.append(quad + two * pair_b)
    out.append(out[6] + one * states[6])
    return out


def kernel(
    q_hbm, k_hbm, v_hbm, table, head_table, gain, out_ref,
    q, k, v, comb, leaf_state, local, own, xrecv, total, zrecv, csend, carry, dsend, far, ssq, ssq_in,
    in_sem, x_send, x_recv, z_send, z_recv, c_send, c_recv, d_send, d_recv, s_send, s_recv,
):
    head = lax.axis_index("head")
    ctx = lax.axis_index("ctx")
    x = lax.rem(ctx, NX)
    z = lax.div(ctx, NX)

    def in_copy(i, src, dst, j):
        rows = pl.ds(pl.multiple_of(j * LEAF, LEAF), LEAF)
        return pltpu.make_async_copy(src.at[rows], dst.at[rows], in_sem.at[i, j])

    for j in range(LEAVES):
        in_copy(0, k_hbm, k, j).start()
        in_copy(1, v_hbm, v, j).start()
    for j in range(LEAVES):
        in_copy(2, q_hbm, q, j).start()

    barrier = pltpu.get_barrier_semaphore()
    for d in range(1, NX):
        pl.semaphore_signal(barrier, 1, device_id={"ctx": z * NX + lax.rem(x + d, NX)}, device_id_type=MESH)
    for d in range(1, NZ):
        pl.semaphore_signal(barrier, 1, device_id={"ctx": lax.rem(z + d, NZ) * NX + x}, device_id_type=MESH)
    for d in range(1, NH):
        pl.semaphore_signal(barrier, 1, device_id={"head": lax.rem(head + d, NH)}, device_id_type=MESH)

    def weight(h, level):
        return table[head_table[head * HEADS_HERE + h], level] * SCALES[level]

    def leaf_states(j, _):
        in_copy(0, k_hbm, k, j).wait()
        in_copy(1, v_hbm, v, j).wait()
        rows = pl.ds(pl.multiple_of(j * LEAF, LEAF), LEAF)
        for p in range(HEADS_HERE // 2):
            columns = slice(p * 256, p * 256 + 256)
            both = dot(k[rows, columns], v[rows, columns], TN)
            leaf_state[j, 2 * p] = both[:HEAD_DIM, :HEAD_DIM]
            leaf_state[j, 2 * p + 1] = both[HEAD_DIM:, HEAD_DIM:]
        return 0

    lax.fori_loop(0, LEAVES, leaf_states, 0)
    for h in range(HEADS_HERE):
        s = [leaf_state[j, h] for j in range(LEAVES)]
        own[h] = ((s[0] + s[1]) + (s[2] + s[3])) + ((s[4] + s[5]) + (s[6] + s[7]))

    pl.semaphore_wait(barrier, NX + NZ + NH - 3)

    def x_copy(d):
        to = lax.rem(x + d, NX)
        return pltpu.make_async_remote_copy(
            own.at[to], xrecv.at[x], x_send.at[d], x_recv.at[d],
            device_id={"ctx": z * NX + to}, device_id_type=MESH)

    def z_copy(d):
        to = lax.rem(z + d, NZ)
        return pltpu.make_async_remote_copy(
            total.at[pl.ds(pl.multiple_of(to * SLICE, SLICE), SLICE)], zrecv.at[z], z_send.at[d], z_recv.at[d],
            device_id={"ctx": to * NX + x}, device_id_type=MESH)

    def c_copy(d):
        to = lax.rem(z + d, NZ)
        return pltpu.make_async_remote_copy(
            csend.at[to], carry.at[pl.ds(pl.multiple_of(z * SLICE, SLICE), SLICE)], c_send.at[d], c_recv.at[d],
            device_id={"ctx": to * NX + x}, device_id_type=MESH)

    def d_copy(d):
        to = lax.rem(x + d, NX)
        return pltpu.make_async_remote_copy(
            dsend.at[to], far.at[x], d_send.at[d], d_recv.at[d],
            device_id={"ctx": z * NX + to}, device_id_type=MESH)

    for d in (2, 1, 3):
        x_copy(d).start()
    xrecv[x] = own[x]

    for h in range(HEADS_HERE):
        s = [leaf_state[j, h] for j in range(LEAVES)]
        sums = fenwick(s, weight(h, 1), weight(h, 2), weight(h, 3))
        local[0, h] = jnp.zeros((HEAD_DIM, HEAD_DIM), jnp.bfloat16)
        for j in range(1, LEAVES):
            local[j, h] = sums[j].astype(jnp.bfloat16)

    causal = lax.broadcasted_iota(jnp.int32, (LEAF, LEAF), 1) <= lax.broadcasted_iota(jnp.int32, (LEAF, LEAF), 0)

    def near(j, _):
        in_copy(2, q_hbm, q, j).wait()
        rows = pl.ds(pl.multiple_of(j * LEAF, LEAF), LEAF)
        for h in range(HEADS_HERE):
            columns = slice(h * HEAD_DIM, (h + 1) * HEAD_DIM)
            qs = q[rows, columns]
            scores = dot(qs, k[rows, columns], NT)
            rounded = jnp.where(causal, scores * weight(h, 0), 0.0).astype(jnp.bfloat16)
            comb[rows, columns] = dot(rounded, v[rows, columns]) + dot(qs, local[j, h])
        return 0

    lax.fori_loop(0, 3, near, 0)

    for d in range(1, NX):
        x_copy(d).wait_recv()
    total[...] = (xrecv[0] + xrecv[1]) + (xrecv[2] + xrecv[3])
    for d in (4, 3, 5, 2, 6, 1, 7):
        z_copy(d).start()
    zrecv[z] = total[pl.ds(pl.multiple_of(z * SLICE, SLICE), SLICE), :]

    lax.fori_loop(3, 5, near, 0)

    for d in range(1, NZ):
        z_copy(d).wait_recv()
    sums = fenwick([zrecv[i] for i in range(NZ)], weight(x, 6), weight(x, 7), weight(x, 8))
    csend[0] = jnp.zeros((SLICE, HEAD_DIM), jnp.float32)
    for i in range(1, NZ):
        csend[i] = sums[i]
    for d in (4, 3, 5, 2, 6, 1, 7):
        c_copy(d).start()
    carry[pl.ds(pl.multiple_of(z * SLICE, SLICE), SLICE), :] = csend[z]

    lax.fori_loop(5, 7, near, 0)

    for d in range(1, NZ):
        c_copy(d).wait_recv()
    sums = fenwick([xrecv[i] for i in range(NX)], weight(x, 4), weight(x, 5))
    dsend[0] = carry[...]
    for i in range(1, NX):
        dsend[i] = carry[...] + sums[i]
    for d in (2, 1, 3):
        d_copy(d).start()
    far[x] = dsend[x]

    lax.fori_loop(7, LEAVES, near, 0)

    for d in range(1, NX):
        d_copy(d).wait_recv()

    zero = jnp.zeros((HEAD_DIM, HEAD_DIM), jnp.float32)
    high, low = [], []
    for p in range(HEADS_HERE // 2):
        block = jnp.concatenate([
            jnp.concatenate([far[2 * p], zero], axis=1),
            jnp.concatenate([zero, far[2 * p + 1]], axis=1)], axis=0)
        top = block.astype(jnp.bfloat16)
        high.append(top)
        low.append((block - top.astype(jnp.float32)).astype(jnp.bfloat16))
    ones = jnp.ones((8, HEAD_DIM), jnp.bfloat16)

    def s_copy(c, d):
        return pltpu.make_async_remote_copy(
            ssq.at[c], ssq_in.at[c, d], s_send.at[c, d], s_recv.at[c, d],
            device_id={"head": lax.rem(head + d, NH)}, device_id_type=MESH)

    for c in range(CHUNKS):
        for j in range(ROWS // LEAF):
            rows = slice(c * ROWS + j * LEAF, c * ROWS + (j + 1) * LEAF)
            squares = None
            for p in range(HEADS_HERE // 2):
                columns = slice(p * 256, p * 256 + 256)
                qs = q[rows, columns]
                value = comb[rows, columns] + (dot(qs, high[p]) + dot(qs, low[p]))
                comb[rows, columns] = value
                square = value * value
                square = square[:, :HEAD_DIM] + square[:, HEAD_DIM:]
                squares = square if squares is None else squares + square
            top = squares.astype(jnp.bfloat16)
            rest = (squares - top.astype(jnp.float32)).astype(jnp.bfloat16)
            line = dot(ones, top, NT) + dot(ones, rest, NT)
            ssq[c, 2 * j:2 * j + 1] = line[:1, :HEAD_DIM]
            ssq[c, 2 * j + 1:2 * j + 2] = line[:1, HEAD_DIM:]
        for d in range(1, NH):
            s_copy(c, d).start()

    for c in range(CHUNKS):
        for d in range(1, NH):
            s_copy(c, d).wait_recv()
        a = [ssq[c]] + [ssq_in[c, d] for d in range(1, NH)]
        whole = ((a[0] + a[1]) + (a[2] + a[3])) + ((a[4] + a[5]) + (a[6] + a[7]))
        inverse = lax.rsqrt(whole * (1.0 / D) + EPSILON).T
        for i in range(ROWS // HEAD_DIM):
            rows = slice(c * ROWS + i * HEAD_DIM, c * ROWS + (i + 1) * HEAD_DIM)
            out_ref[rows] = (comb[rows] * inverse[:, i:i + 1] * gain[...]).astype(jnp.bfloat16)

    for d in range(1, NX):
        x_copy(d).wait_send()
        d_copy(d).wait_send()
    for d in range(1, NZ):
        z_copy(d).wait_send()
        c_copy(d).wait_send()
    for c in range(CHUNKS):
        for d in range(1, NH):
            s_copy(c, d).wait_send()


def shards(queries, keys, values, level_table, head_table, gain):
    f32, bf16 = jnp.float32, jnp.bfloat16
    dma = pltpu.SemaphoreType.DMA
    square = (HEAD_DIM, HEAD_DIM)
    anywhere = pl.BlockSpec(memory_space=pltpu.HBM)
    smem = pl.BlockSpec(memory_space=pltpu.SMEM)
    vmem = pl.BlockSpec(memory_space=pltpu.VMEM)
    return pl.pallas_call(
        kernel,
        out_shape=jax.ShapeDtypeStruct((SEG, WIDTH), bf16),
        in_specs=[anywhere, anywhere, anywhere, smem, smem, vmem],
        out_specs=vmem,
        scratch_shapes=[
            pltpu.VMEM((SEG, WIDTH), bf16),
            pltpu.VMEM((SEG, WIDTH), bf16),
            pltpu.VMEM((SEG, WIDTH), bf16),
            pltpu.VMEM((SEG, WIDTH), f32),
            pltpu.VMEM((LEAVES, HEADS_HERE, *square), f32),
            pltpu.VMEM((LEAVES, HEADS_HERE, *square), bf16),
            pltpu.VMEM((HEADS_HERE, *square), f32),
            pltpu.VMEM((NX, *square), f32),
            pltpu.VMEM(square, f32),
            pltpu.VMEM((NZ, SLICE, HEAD_DIM), f32),
            pltpu.VMEM((NZ, SLICE, HEAD_DIM), f32),
            pltpu.VMEM(square, f32),
            pltpu.VMEM((NX, *square), f32),
            pltpu.VMEM((HEADS_HERE, *square), f32),
            pltpu.VMEM((CHUNKS, 8, HEAD_DIM), f32),
            pltpu.VMEM((CHUNKS, NH, 8, HEAD_DIM), f32),
            dma((3, LEAVES)),
            dma((NX,)), dma((NX,)),
            dma((NZ,)), dma((NZ,)),
            dma((NZ,)), dma((NZ,)),
            dma((NX,)), dma((NX,)),
            dma((CHUNKS, NH)), dma((CHUNKS, NH)),
        ],
        compiler_params=pltpu.CompilerParams(
            collective_id=0, has_side_effects=True, vmem_limit_bytes=40 * 1024 * 1024),
        name="attend",
    )(queries, keys, values, level_table, head_table, gain.reshape(1, WIDTH))


def solution(mesh):
    return jax.shard_map(
        shards,
        mesh=mesh,
        in_specs=(P("ctx", "head"), P("ctx", "head"), P("ctx", "head"), P(), P(), P("head")),
        out_specs=P("ctx", "head"),
        check_vma=False,
    )
```

```python
import functools

import jax
import jax.numpy as jnp
import numpy as np
from jax import lax
from jax.experimental import pallas as pl
from jax.experimental.pallas import tpu as pltpu
from jax.sharding import PartitionSpec as P

HEAD_DIM = 128
LEAF = 256
LEAVES = 8
D = 4096
HEADS_HERE = 4
SEG = LEAF * LEAVES
WIDTH = HEADS_HERE * HEAD_DIM
NX, GROUPS, NH = 4, 4, 8
HALF = HEAD_DIM // 2
AROUND = [(1, 2), (1, 1), (1, 3), (0, 2), (1, 0), (0, 1), (0, 3)]
CHUNKS = 2
ROWS = SEG // CHUNKS
EPSILON = 1e-06
MESH = pl.DeviceIdType.MESH
SCALES = [float(np.float32(1.0) / np.sqrt(np.float32(LEAF * 2 ** max(l - 1, 0)))) for l in range(9)]

NT = (((1,), (1,)), ((), ()))
TN = (((0,), (0,)), ((), ()))


def dot(a, b, dims=(((1,), (0,)), ((), ()))):
    return lax.dot_general(a, b, dims, preferred_element_type=jnp.float32)


def fenwick(states, one, two, four=None):
    out = []
    pair = states[0] + states[1]
    out.append(None)
    out.append(one * states[0])
    out.append(two * pair)
    out.append(out[2] + one * states[2])
    if four is None:
        return out
    pair_b = states[4] + states[5]
    quad = four * (pair + (states[2] + states[3]))
    out.append(quad)
    out.append(quad + one * states[4])
    out.append(quad + two * pair_b)
    out.append(out[6] + one * states[6])
    return out


def kernel(
    q_hbm, k_hbm, v_hbm, table, head_table, gain, out_ref,
    q, k, v, comb, leaf_state, local, own, xrecv, total, earlier, dsend, far, ssq, ssq_in,
    in_sem, x_send, x_recv, t_send, t_recv, d_send, d_recv, s_send, s_recv, ready,
):
    head = lax.axis_index("head")
    ctx = lax.axis_index("ctx")
    x = lax.rem(ctx, NX)
    z = lax.div(ctx, NX)
    group = lax.div(z, 2)
    odd = lax.rem(z, 2)
    part = lax.rem(odd + lax.div(z, 4), 2)

    def in_copy(i, src, dst, j):
        rows = pl.ds(pl.multiple_of(j * LEAF, LEAF), LEAF)
        return pltpu.make_async_copy(src.at[rows], dst.at[rows], in_sem.at[i, j])

    for j in range(LEAVES):
        in_copy(0, k_hbm, k, j).start()
        in_copy(1, v_hbm, v, j).start()

    def near_by(dz, dx):
        to_odd, to_x = lax.rem(odd + dz, 2), lax.rem(x + dx, NX)
        return to_odd, to_x, {"ctx": (2 * group + to_odd) * NX + to_x}

    def counterpart(g):
        return {"ctx": (2 * g + lax.rem(part + g // 2, 2)) * NX + x}

    for g in range(GROUPS - 1):
        earlier[g] = jnp.zeros((HALF, HEAD_DIM), jnp.float32)
    barrier = pltpu.get_barrier_semaphore()
    for dz, dx in AROUND:
        pl.semaphore_signal(barrier, 1, device_id=near_by(dz, dx)[2], device_id_type=MESH)
    for g in range(1, GROUPS):
        @pl.when(group < g)
        def _():
            pl.semaphore_signal(barrier, 1, device_id=counterpart(g), device_id_type=MESH)
    for d in range(1, NH):
        pl.semaphore_signal(barrier, 1, device_id={"head": lax.rem(head + d, NH)}, device_id_type=MESH)

    def weight(h, level):
        return table[head_table[head * HEADS_HERE + h], level] * SCALES[level]

    def leaf_states(j, _):
        in_copy(0, k_hbm, k, j).wait()
        in_copy(1, v_hbm, v, j).wait()
        rows = pl.ds(pl.multiple_of(j * LEAF, LEAF), LEAF)
        for p in range(HEADS_HERE // 2):
            columns = slice(p * 256, p * 256 + 256)
            both = dot(k[rows, columns], v[rows, columns], TN)
            leaf_state[j, 2 * p] = both[:HEAD_DIM, :HEAD_DIM]
            leaf_state[j, 2 * p + 1] = both[HEAD_DIM:, HEAD_DIM:]
        return 0

    lax.fori_loop(0, LEAVES, leaf_states, 0)
    for h in range(HEADS_HERE):
        s = [leaf_state[j, h] for j in range(LEAVES)]
        whole = ((s[0] + s[1]) + (s[2] + s[3])) + ((s[4] + s[5]) + (s[6] + s[7]))
        own[h, 0] = whole[:HALF]
        own[h, 1] = whole[HALF:]

    pl.semaphore_wait(barrier, len(AROUND) + NH - 1 + group)
    for g in range(GROUPS - 1):
        @pl.when(group > g)
        def _():
            pl.semaphore_signal(ready.at[group], 1, device_id=counterpart(g), device_id_type=MESH)

    def x_copy(dz, dx):
        to_odd, to_x, to = near_by(dz, dx)
        return pltpu.make_async_remote_copy(
            own.at[to_x, lax.rem(to_odd + lax.div(z, 4), 2)], xrecv.at[odd, x],
            x_send.at[dz, dx], x_recv.at[dz, dx], device_id=to, device_id_type=MESH)

    def t_copy(g):
        return pltpu.make_async_remote_copy(
            total, earlier.at[group], t_send.at[g], t_recv.at[group],
            device_id=counterpart(g), device_id_type=MESH)

    def t_arrival(g):
        return pltpu.make_async_remote_copy(
            total, earlier.at[g], t_send.at[g], t_recv.at[g],
            device_id=counterpart(g), device_id_type=MESH)

    def d_copy(dz, dx):
        to_odd, to_x, to = near_by(dz, dx)
        return pltpu.make_async_remote_copy(
            dsend.at[to_odd, to_x], far.at[x, part],
            d_send.at[dz, dx], d_recv.at[dz, dx], device_id=to, device_id_type=MESH)

    for dz, dx in AROUND:
        x_copy(dz, dx).start()
    xrecv[odd, x] = own[x, part]
    for j in range(LEAVES):
        in_copy(2, q_hbm, q, j).start()

    for h in range(HEADS_HERE):
        s = [leaf_state[j, h] for j in range(LEAVES)]
        sums = fenwick(s, weight(h, 1), weight(h, 2), weight(h, 3))
        local[0, h] = jnp.zeros((HEAD_DIM, HEAD_DIM), jnp.bfloat16)
        for j in range(1, LEAVES):
            local[j, h] = sums[j].astype(jnp.bfloat16)

    causal = lax.broadcasted_iota(jnp.int32, (LEAF, LEAF), 1) <= lax.broadcasted_iota(jnp.int32, (LEAF, LEAF), 0)

    def near(j, _):
        in_copy(2, q_hbm, q, j).wait()
        rows = pl.ds(pl.multiple_of(j * LEAF, LEAF), LEAF)
        for h in range(HEADS_HERE):
            columns = slice(h * HEAD_DIM, (h + 1) * HEAD_DIM)
            qs = q[rows, columns]
            scores = dot(qs, k[rows, columns], NT)
            rounded = jnp.where(causal, scores * weight(h, 0), 0.0).astype(jnp.bfloat16)
            comb[rows, columns] = dot(rounded, v[rows, columns]) + dot(qs, local[j, h])
        return 0

    lax.fori_loop(0, 3, near, 0)

    for dz, dx in AROUND:
        x_copy(dz, dx).wait_recv()
    row = [[xrecv[i, j] for j in range(NX)] for i in range(2)]
    row_sum = [(r[0] + r[1]) + (r[2] + r[3]) for r in row]
    total[...] = row_sum[0] + row_sum[1]
    for g in range(GROUPS - 1, 0, -1):
        @pl.when(group < g)
        def _():
            pl.semaphore_wait(ready.at[g], 1)
            t_copy(g).start()

    lax.fori_loop(3, 5, near, 0)

    for g in range(GROUPS - 1):
        @pl.when(group > g)
        def _():
            t_arrival(g).wait_recv()
    far_weight = jnp.where(group >= 2, weight(x, 8), 0.0)
    base = (
        (far_weight + jnp.where(group == 1, weight(x, 7), 0.0)) * earlier[0]
        + far_weight * earlier[1]
        + jnp.where(group == 3, weight(x, 7), 0.0) * earlier[2])
    for i in range(2):
        sums = fenwick(row[i], weight(x, 4), weight(x, 5))
        if i:
            base = base + weight(x, 6) * row_sum[0]
        dsend[i, 0] = base
        for j in range(1, NX):
            dsend[i, j] = base + sums[j]
    for dz, dx in AROUND:
        d_copy(dz, dx).start()
    far[x, part] = dsend[odd, x]

    lax.fori_loop(5, LEAVES, near, 0)

    for dz, dx in AROUND:
        d_copy(dz, dx).wait_recv()

    zero = jnp.zeros((HEAD_DIM, HEAD_DIM), jnp.float32)
    high, low = [], []
    state = [jnp.concatenate([far[h, 0], far[h, 1]], axis=0) for h in range(HEADS_HERE)]
    for p in range(HEADS_HERE // 2):
        block = jnp.concatenate([
            jnp.concatenate([state[2 * p], zero], axis=1),
            jnp.concatenate([zero, state[2 * p + 1]], axis=1)], axis=0)
        top = block.astype(jnp.bfloat16)
        high.append(top)
        low.append((block - top.astype(jnp.float32)).astype(jnp.bfloat16))
    ones = jnp.ones((8, HEAD_DIM), jnp.bfloat16)

    def s_copy(c, d):
        return pltpu.make_async_remote_copy(
            ssq.at[c], ssq_in.at[c, d], s_send.at[c, d], s_recv.at[c, d],
            device_id={"head": lax.rem(head + d, NH)}, device_id_type=MESH)

    for c in range(CHUNKS):
        for j in range(ROWS // LEAF):
            rows = slice(c * ROWS + j * LEAF, c * ROWS + (j + 1) * LEAF)
            squares = None
            for p in range(HEADS_HERE // 2):
                columns = slice(p * 256, p * 256 + 256)
                qs = q[rows, columns]
                value = comb[rows, columns] + (dot(qs, high[p]) + dot(qs, low[p]))
                comb[rows, columns] = value
                square = value * value
                square = square[:, :HEAD_DIM] + square[:, HEAD_DIM:]
                squares = square if squares is None else squares + square
            top = squares.astype(jnp.bfloat16)
            rest = (squares - top.astype(jnp.float32)).astype(jnp.bfloat16)
            line = dot(ones, top, NT) + dot(ones, rest, NT)
            ssq[c, 2 * j:2 * j + 1] = line[:1, :HEAD_DIM]
            ssq[c, 2 * j + 1:2 * j + 2] = line[:1, HEAD_DIM:]
        for d in range(1, NH):
            s_copy(c, d).start()

    for c in range(CHUNKS):
        for d in range(1, NH):
            s_copy(c, d).wait_recv()
        a = [ssq[c]] + [ssq_in[c, d] for d in range(1, NH)]
        whole = ((a[0] + a[1]) + (a[2] + a[3])) + ((a[4] + a[5]) + (a[6] + a[7]))
        inverse = lax.rsqrt(whole * (1.0 / D) + EPSILON).T
        for i in range(ROWS // HEAD_DIM):
            rows = slice(c * ROWS + i * HEAD_DIM, c * ROWS + (i + 1) * HEAD_DIM)
            out_ref[rows] = (comb[rows] * inverse[:, i:i + 1] * gain[...]).astype(jnp.bfloat16)

    for dz, dx in AROUND:
        x_copy(dz, dx).wait_send()
        d_copy(dz, dx).wait_send()
    for g in range(1, GROUPS):
        @pl.when(group < g)
        def _():
            t_copy(g).wait_send()
    for c in range(CHUNKS):
        for d in range(1, NH):
            s_copy(c, d).wait_send()


def shards(queries, keys, values, level_table, head_table, gain):
    f32, bf16 = jnp.float32, jnp.bfloat16
    dma = pltpu.SemaphoreType.DMA
    square, half = (HEAD_DIM, HEAD_DIM), (HALF, HEAD_DIM)
    anywhere = pl.BlockSpec(memory_space=pltpu.HBM)
    smem = pl.BlockSpec(memory_space=pltpu.SMEM)
    vmem = pl.BlockSpec(memory_space=pltpu.VMEM)
    return pl.pallas_call(
        kernel,
        out_shape=pltpu.VMEM((SEG, WIDTH), bf16),
        in_specs=[anywhere, anywhere, anywhere, smem, smem, vmem],
        out_specs=vmem,
        scratch_shapes=[
            pltpu.VMEM((SEG, WIDTH), bf16),
            pltpu.VMEM((SEG, WIDTH), bf16),
            pltpu.VMEM((SEG, WIDTH), bf16),
            pltpu.VMEM((SEG, WIDTH), f32),
            pltpu.VMEM((LEAVES, HEADS_HERE, *square), f32),
            pltpu.VMEM((LEAVES, HEADS_HERE, *square), bf16),
            pltpu.VMEM((HEADS_HERE, 2, *half), f32),
            pltpu.VMEM((2, NX, *half), f32),
            pltpu.VMEM(half, f32),
            pltpu.VMEM((GROUPS - 1, *half), f32),
            pltpu.VMEM((2, NX, *half), f32),
            pltpu.VMEM((HEADS_HERE, 2, *half), f32),
            pltpu.VMEM((CHUNKS, 8, HEAD_DIM), f32),
            pltpu.VMEM((CHUNKS, NH, 8, HEAD_DIM), f32),
            dma((3, LEAVES)),
            dma((2, NX)), dma((2, NX)),
            dma((GROUPS,)), dma((GROUPS,)),
            dma((2, NX)), dma((2, NX)),
            dma((CHUNKS, NH)), dma((CHUNKS, NH)),
            pltpu.SemaphoreType.REGULAR((GROUPS,)),
        ],
        compiler_params=pltpu.CompilerParams(
            collective_id=0, has_side_effects=True, vmem_limit_bytes=40 * 1024 * 1024),
        name="attend",
    )(*[pltpu.with_memory_space_constraint(a, pltpu.HBM) for a in
       (queries, keys, values, level_table, head_table, gain.reshape(1, WIDTH))])


def solution(mesh):
    return jax.shard_map(
        shards,
        mesh=mesh,
        in_specs=(P("ctx", "head"), P("ctx", "head"), P("ctx", "head"), P(), P(), P("head")),
        out_specs=P("ctx", "head"),
        check_vma=False,
    )
```

```python
import functools

import jax
import jax.numpy as jnp
import numpy as np
from jax import lax
from jax.experimental import pallas as pl
from jax.experimental.pallas import tpu as pltpu
from jax.sharding import PartitionSpec as P

HEAD_DIM = 128
LEAF = 256
LEAVES = 8
D = 4096
HEADS_HERE = 4
SEG = LEAF * LEAVES
WIDTH = HEADS_HERE * HEAD_DIM
NX, GROUPS, NH = 4, 4, 8
HALF = HEAD_DIM // 2
PAIR = 2 * HEAD_DIM
CHUNK = 2 * LEAF
AROUND = [(1, 2), (1, 1), (1, 3), (0, 2), (1, 0), (0, 1), (0, 3)]
CHUNKS = 2
ROWS = SEG // CHUNKS
EPSILON = 1e-06
MESH = pl.DeviceIdType.MESH
SCALES = [float(np.float32(1.0) / np.sqrt(np.float32(LEAF * 2 ** max(l - 1, 0)))) for l in range(9)]

NT = (((1,), (1,)), ((), ()))
TN = (((0,), (0,)), ((), ()))


def dot(a, b, dims=(((1,), (0,)), ((), ()))):
    return lax.dot_general(a, b, dims, preferred_element_type=jnp.float32)


def fenwick(states, one, two, four=None):
    out = []
    pair = states[0] + states[1]
    out.append(None)
    out.append(one * states[0])
    out.append(two * pair)
    out.append(out[2] + one * states[2])
    if four is None:
        return out
    pair_b = states[4] + states[5]
    quad = four * (pair + (states[2] + states[3]))
    out.append(quad)
    out.append(quad + one * states[4])
    out.append(quad + two * pair_b)
    out.append(out[6] + one * states[6])
    return out


def kernel(
    q_hbm, k_hbm, v_hbm, table_hbm, head_table_hbm, gain_hbm, out_ref,
    table, head_table, gain, q, kv, comb, square_sum, leaf_state, local, own, xrecv, total, earlier, dsend, far,
    ssq, ssq_in, small_sem, kv_sem, q_sem, x_send, x_recv, t_send, t_recv, d_send, d_recv, s_send, s_recv, ready,
):
    head = lax.axis_index("head")
    ctx = lax.axis_index("ctx")
    x = lax.rem(ctx, NX)
    z = lax.div(ctx, NX)
    group = lax.div(z, 2)
    odd = lax.rem(z, 2)
    part = lax.rem(odd + lax.div(z, 4), 2)

    def kv_part(p, c):
        return pl.ds(c * CHUNK, CHUNK), pl.ds(p * PAIR, PAIR)

    for p in range(HEADS_HERE // 2):
        for c in range(SEG // CHUNK):
            here = kv_part(p, c)
            pltpu.make_async_copy(k_hbm.at[here], kv.at[(0, *here)], kv_sem.at[p, c]).start()
            pltpu.make_async_copy(v_hbm.at[here], kv.at[(1, *here)], kv_sem.at[p, c]).start()
    small = [
        pltpu.make_async_copy(a, b, small_sem.at[i])
        for i, (a, b) in enumerate(((table_hbm, table), (head_table_hbm, head_table), (gain_hbm, gain)))]
    for copy in small:
        copy.start()
    q_copy = pltpu.make_async_copy(q_hbm, q, q_sem)

    def near_by(dz, dx):
        to_odd, to_x = lax.rem(odd + dz, 2), lax.rem(x + dx, NX)
        return to_odd, to_x, {"ctx": (2 * group + to_odd) * NX + to_x}

    def counterpart(g):
        return {"ctx": (2 * g + lax.rem(part + g // 2, 2)) * NX + x}

    for g in range(GROUPS - 1):
        earlier[g] = jnp.zeros((HALF, HEAD_DIM), jnp.float32)
    barrier = pltpu.get_barrier_semaphore()
    for dz, dx in AROUND:
        pl.semaphore_signal(barrier, 1, device_id=near_by(dz, dx)[2], device_id_type=MESH)
    for g in range(1, GROUPS):
        @pl.when(group < g)
        def _():
            pl.semaphore_signal(barrier, 1, device_id=counterpart(g), device_id_type=MESH)
    for d in range(1, NH):
        pl.semaphore_signal(barrier, 1, device_id={"head": lax.rem(head + d, NH)}, device_id_type=MESH)

    def weight(h, level):
        return table[head_table[head * HEADS_HERE + h], level] * SCALES[level]

    def x_copy(dz, dx):
        to_odd, to_x, to = near_by(dz, dx)
        return pltpu.make_async_remote_copy(
            own.at[to_x, lax.rem(to_odd + lax.div(z, 4), 2)], xrecv.at[odd, x],
            x_send, x_recv, device_id=to, device_id_type=MESH)

    def t_copy(g):
        return pltpu.make_async_remote_copy(
            total, earlier.at[group], t_send.at[g - 1], t_recv.at[group],
            device_id=counterpart(g), device_id_type=MESH)

    def d_copy(dz, dx):
        to_odd, to_x, to = near_by(dz, dx)
        return pltpu.make_async_remote_copy(
            dsend.at[to_odd, to_x], far.at[x, part],
            d_send, d_recv.at[dx], device_id=to, device_id_type=MESH)

    def pair_states(p):
        columns = slice(p * PAIR, (p + 1) * PAIR)
        whole = None
        for c in range(SEG // CHUNK):
            arrived = kv.at[(slice(None), *kv_part(p, c))]
            pltpu.make_async_copy(arrived, arrived, kv_sem.at[p, c]).wait()
            for j in range(c * CHUNK // LEAF, (c + 1) * CHUNK // LEAF):
                rows = slice(j * LEAF, (j + 1) * LEAF)
                both = dot(kv[0, rows, columns], kv[1, rows, columns], TN)
                two = both[:HEAD_DIM, :HEAD_DIM], both[HEAD_DIM:, HEAD_DIM:]
                for i in range(2):
                    leaf_state[j, 2 * p + i] = two[i]
                whole = two if whole is None else [m + n for m, n in zip(whole, two)]
        for i in range(2):
            own[2 * p + i, 0] = whole[i][:HALF]
            own[2 * p + i, 1] = whole[i][HALF:]
        if p == 0:
            pl.semaphore_wait(barrier, len(AROUND) + NH - 1 + group)
        for dz, dx in AROUND:
            @pl.when(lax.div(near_by(dz, dx)[1], 2) == p)
            def _():
                x_copy(dz, dx).start()

    pair_states(0)
    for g in range(GROUPS - 1):
        @pl.when(group > g)
        def _():
            pl.semaphore_signal(ready.at[group - 1], 1, device_id=counterpart(g), device_id_type=MESH)
    q_copy.start()
    pair_states(1)
    xrecv[odd, x] = own[x, part]
    for copy in small:
        copy.wait()

    for h in range(HEADS_HERE):
        s = [leaf_state[j, h] for j in range(LEAVES)]
        sums = fenwick(s, weight(h, 1), weight(h, 2), weight(h, 3))
        local[0, h] = jnp.zeros((HEAD_DIM, HEAD_DIM), jnp.bfloat16)
        for j in range(1, LEAVES):
            local[j, h] = sums[j].astype(jnp.bfloat16)

    causal = lax.broadcasted_iota(jnp.int32, (LEAF, LEAF), 1) <= lax.broadcasted_iota(jnp.int32, (LEAF, LEAF), 0)

    def near(j, _):
        rows = pl.ds(pl.multiple_of(j * LEAF, LEAF), LEAF)
        for h in range(HEADS_HERE):
            columns = slice(h * HEAD_DIM, (h + 1) * HEAD_DIM)
            qs = q[rows, columns]
            scores = dot(qs, kv[0, rows, columns], NT)
            rounded = jnp.where(causal, scores * weight(h, 0), 0.0).astype(jnp.bfloat16)
            comb[h, rows] = dot(rounded, kv[1, rows, columns]) + dot(qs, local[j, h])
        return 0

    q_copy.wait()
    lax.fori_loop(0, 3, near, 0)

    def all_but_one(ref, sem):
        seven = ref.at[pl.ds(0, len(AROUND))]
        return pltpu.make_async_copy(seven, seven, sem)

    all_but_one(xrecv.reshape(2 * NX, HALF, HEAD_DIM), x_recv).wait()
    row = [[xrecv[i, j] for j in range(NX)] for i in range(2)]
    row_sum = [(r[0] + r[1]) + (r[2] + r[3]) for r in row]
    total[...] = row_sum[0] + row_sum[1]
    for g in range(GROUPS - 1, 0, -1):
        @pl.when(group < g)
        def _():
            pl.semaphore_wait(ready.at[g - 1], 1)
            t_copy(g).start()

    reached = jnp.where(group == GROUPS - 1, 4, 3)
    lax.fori_loop(3, reached, near, 0)

    for g in range(GROUPS - 1):
        @pl.when(group > g)
        def _():
            pltpu.make_async_copy(earlier.at[g], earlier.at[g], t_recv.at[g]).wait()
    far_weight = jnp.where(group >= 2, weight(x, 8), 0.0)
    base = (
        (far_weight + jnp.where(group == 1, weight(x, 7), 0.0)) * earlier[0]
        + far_weight * earlier[1]
        + jnp.where(group == 3, weight(x, 7), 0.0) * earlier[2])
    for i in range(2):
        sums = fenwick(row[i], weight(x, 4), weight(x, 5))
        if i:
            base = base + weight(x, 6) * row_sum[0]
        dsend[i, 0] = base
        for j in range(1, NX):
            dsend[i, j] = base + sums[j]
    for dz, dx in AROUND:
        d_copy(dz, dx).start()
    far[x, part] = dsend[odd, x]

    lax.fori_loop(reached, LEAVES, near, 0)

    def s_copy(c, d):
        return pltpu.make_async_remote_copy(
            ssq.at[c], ssq_in.at[c, d - 1], s_send.at[c], s_recv.at[c],
            device_id={"head": lax.rem(head + d, NH)}, device_id_type=MESH)

    ones = jnp.ones((8, 2 * HEAD_DIM), jnp.bfloat16)
    order = (0, 1, 3, 2)
    for dx in order:
        h = lax.rem(x + NX - dx, NX)
        arrived = far.at[h] if dx else far.at[h, part]
        pltpu.make_async_copy(arrived, arrived, d_recv.at[dx]).wait()
        state = jnp.concatenate([far[h, 0], far[h, 1]], axis=0)
        state = state.astype(jnp.bfloat16)
        columns = pl.ds(pl.multiple_of(h * HEAD_DIM, HEAD_DIM), HEAD_DIM)
        for j in range(LEAVES):
            rows = slice(j * LEAF, (j + 1) * LEAF)
            if j % 4 == 0:
                qs = q[j * LEAF:(j + 4) * LEAF, columns]
                both = dot(qs, state)
            value = comb[h, rows] + both[j % 4 * LEAF:(j % 4 + 1) * LEAF]
            comb[h, rows] = value
            squares = value * value
            if dx != order[0]:
                squares = squares + square_sum[rows]
            if dx != order[-1]:
                square_sum[rows] = squares
                continue
            top = squares.astype(jnp.bfloat16)
            rest = (squares - top.astype(jnp.float32)).astype(jnp.bfloat16)
            line = dot(ones, jnp.concatenate([top, rest], axis=1), NT)
            c, i = divmod(j, LEAVES // CHUNKS)
            ssq[c, 2 * i:2 * i + 1] = line[:1, :HEAD_DIM]
            ssq[c, 2 * i + 1:2 * i + 2] = line[:1, HEAD_DIM:]
            if i == LEAVES // CHUNKS - 1:
                for d in range(1, NH):
                    s_copy(c, d).start()

    for c in range(CHUNKS):
        pltpu.make_async_copy(ssq_in.at[c], ssq_in.at[c], s_recv.at[c]).wait()
        a = [ssq[c]] + [ssq_in[c, d] for d in range(NH - 1)]
        whole = ((a[0] + a[1]) + (a[2] + a[3])) + ((a[4] + a[5]) + (a[6] + a[7]))
        inverse = lax.rsqrt(whole * (1.0 / D) + EPSILON).T
        for i in range(ROWS // HEAD_DIM):
            rows = slice(c * ROWS + i * HEAD_DIM, c * ROWS + (i + 1) * HEAD_DIM)
            for h in range(HEADS_HERE):
                columns = slice(h * HEAD_DIM, (h + 1) * HEAD_DIM)
                out_ref[rows, columns] = (
                    comb[h, rows] * inverse[:, i:i + 1] * gain[:, columns]).astype(jnp.bfloat16)

    all_but_one(own.reshape(2 * NX, HALF, HEAD_DIM), x_send).wait()
    all_but_one(dsend.reshape(2 * NX, HALF, HEAD_DIM), d_send).wait()
    for g in range(1, GROUPS):
        @pl.when(group < g)
        def _():
            t_copy(g).wait_send()
    for c in range(CHUNKS):
        pltpu.make_async_copy(ssq_in.at[c], ssq_in.at[c], s_send.at[c]).wait()


def shards(queries, keys, values, level_table, head_table, gain):
    f32, bf16 = jnp.float32, jnp.bfloat16
    dma = pltpu.SemaphoreType.DMA
    square, half = (HEAD_DIM, HEAD_DIM), (HALF, HEAD_DIM)
    anywhere = pl.BlockSpec(memory_space=pltpu.HBM)
    vmem = pl.BlockSpec(memory_space=pltpu.VMEM)
    return pl.pallas_call(
        kernel,
        out_shape=pltpu.VMEM((SEG, WIDTH), bf16),
        in_specs=[anywhere] * 6,
        out_specs=vmem,
        scratch_shapes=[
            pltpu.SMEM(level_table.shape, f32),
            pltpu.SMEM(head_table.shape, jnp.int32),
            pltpu.VMEM((1, WIDTH), f32),
            pltpu.VMEM((SEG, WIDTH), bf16),
            pltpu.VMEM((2, SEG, WIDTH), bf16),
            pltpu.VMEM((HEADS_HERE, SEG, HEAD_DIM), f32),
            pltpu.VMEM((SEG, HEAD_DIM), f32),
            pltpu.VMEM((LEAVES, HEADS_HERE, *square), f32),
            pltpu.VMEM((LEAVES, HEADS_HERE, *square), bf16),
            pltpu.VMEM((HEADS_HERE, 2, *half), f32),
            pltpu.VMEM((2, NX, *half), f32),
            pltpu.VMEM(half, f32),
            pltpu.VMEM((GROUPS - 1, *half), f32),
            pltpu.VMEM((2, NX, *half), f32),
            pltpu.VMEM((HEADS_HERE, 2, *half), f32),
            pltpu.VMEM((CHUNKS, ROWS // HEAD_DIM, HEAD_DIM), f32),
            pltpu.VMEM((CHUNKS, NH - 1, ROWS // HEAD_DIM, HEAD_DIM), f32),
            dma((3,)), dma((HEADS_HERE // 2, SEG // CHUNK)), dma,
            dma, dma,
            dma((GROUPS - 1,)), dma((GROUPS - 1,)),
            dma, dma((NX,)),
            dma((CHUNKS,)), dma((CHUNKS,)),
            pltpu.SemaphoreType.REGULAR((GROUPS - 1,)),
        ],
        compiler_params=pltpu.CompilerParams(
            collective_id=0, has_side_effects=True, vmem_limit_bytes=40 * 1024 * 1024),
        name="attend",
    )(*[pltpu.with_memory_space_constraint(a, pltpu.HBM) for a in
       (queries, keys, values, level_table, head_table, gain.reshape(1, WIDTH))])


def solution(mesh):
    return jax.shard_map(
        shards,
        mesh=mesh,
        in_specs=(P("ctx", "head"), P("ctx", "head"), P("ctx", "head"), P(), P(), P("head")),
        out_specs=P("ctx", "head"),
        check_vma=False,
    )
```

```python
import functools

import jax
import jax.numpy as jnp
import numpy as np
from jax import lax
from jax.experimental import pallas as pl
from jax.experimental.pallas import tpu as pltpu
from jax.sharding import PartitionSpec as P

HEAD_DIM = 128
LEAF = 256
LEAVES = 8
D = 4096
HEADS_HERE = 4
SEG = LEAF * LEAVES
WIDTH = HEADS_HERE * HEAD_DIM
NX, GROUPS, NH = 4, 4, 8
STRIP = HEAD_DIM // 4
PAIR = 2 * HEAD_DIM
CHUNK = 2 * LEAF
AROUND = [(1, 2), (1, 1), (1, 3), (0, 2), (1, 0), (0, 1), (0, 3)]
CHUNKS = 2
ROWS = SEG // CHUNKS
EPSILON = 1e-06
MESH = pl.DeviceIdType.MESH
SCALES = [float(np.float32(1.0) / np.sqrt(np.float32(LEAF * 2 ** max(l - 1, 0)))) for l in range(9)]

NT = (((1,), (1,)), ((), ()))
TN = (((0,), (0,)), ((), ()))


def dot(a, b, dims=(((1,), (0,)), ((), ()))):
    return lax.dot_general(a, b, dims, preferred_element_type=jnp.float32)


def fenwick(states, one, two, four=None):
    out = []
    pair = states[0] + states[1]
    out.append(None)
    out.append(one * states[0])
    out.append(two * pair)
    out.append(out[2] + one * states[2])
    if four is None:
        return out
    pair_b = states[4] + states[5]
    quad = four * (pair + (states[2] + states[3]))
    out.append(quad)
    out.append(quad + one * states[4])
    out.append(quad + two * pair_b)
    out.append(out[6] + one * states[6])
    return out


def kernel(
    q_hbm, k_hbm, v_hbm, table_hbm, head_table_hbm, gain_hbm, out_ref,
    table, head_table, gain, q, kv, comb, square_sum, leaf_state, local, own, xrecv, total, earlier, dsend, far,
    ssq, ssq_in, small_sem, kv_sem, q_sem, x_send, x_recv, t_send, t_recv, d_send, d_recv, s_send, s_recv, ready,
):
    head = lax.axis_index("head")
    ctx = lax.axis_index("ctx")
    x = lax.rem(ctx, NX)
    z = lax.div(ctx, NX)
    group = lax.div(z, 2)
    odd = lax.rem(z, 2)
    part = lax.rem(odd + lax.div(z, 4), 2)

    def kv_part(p, c):
        return pl.ds(c * CHUNK, CHUNK), pl.ds(p * PAIR, PAIR)

    def kv_start(p):
        for c in range(SEG // CHUNK):
            here = kv_part(p, c)
            pltpu.make_async_copy(k_hbm.at[here], kv.at[(0, *here)], kv_sem.at[p, c]).start()
            pltpu.make_async_copy(v_hbm.at[here], kv.at[(1, *here)], kv_sem.at[p, c]).start()

    def near_by(dz, dx):
        to_odd, to_x = lax.rem(odd + dz, 2), lax.rem(x + dx, NX)
        return to_odd, to_x, {"ctx": (2 * group + to_odd) * NX + to_x}

    def counterpart(g):
        return {"ctx": (2 * g + lax.rem(part + g // 2, 2)) * NX + x}

    barrier = pltpu.get_barrier_semaphore()
    for dz, dx in AROUND:
        pl.semaphore_signal(barrier, 1, device_id=near_by(dz, dx)[2], device_id_type=MESH)
    kv_start(0)
    for d in range(1, NH):
        pl.semaphore_signal(barrier, 1, device_id={"head": lax.rem(head + d, NH)}, device_id_type=MESH)
    for g in range(1, GROUPS):
        @pl.when(group < g)
        def _():
            pl.semaphore_signal(barrier, 1, device_id=counterpart(g), device_id_type=MESH)
    kv_start(1)
    small = [
        pltpu.make_async_copy(a, b, small_sem.at[i])
        for i, (a, b) in enumerate(((table_hbm, table), (head_table_hbm, head_table), (gain_hbm, gain)))]
    for copy in small:
        copy.start()
    q_copy = pltpu.make_async_copy(q_hbm, q, q_sem)
    for g in range(GROUPS - 1):
        for p in range(HEADS_HERE // 2):
            earlier[p, g] = jnp.zeros((STRIP, HEAD_DIM), jnp.float32)

    def weight(h, level):
        return table[head_table[head * HEADS_HERE + h], level] * SCALES[level]

    strip = 2 * x + part

    def x_copy(p, dz, dx):
        to_odd, to_x, to = near_by(dz, dx)
        return pltpu.make_async_remote_copy(
            own.at[p, 2 * to_x + lax.rem(to_odd + lax.div(z, 4), 2)], xrecv.at[p, odd, x],
            x_send, x_recv.at[p, odd], device_id=to, device_id_type=MESH)

    def t_copy(p, g):
        return pltpu.make_async_remote_copy(
            total.at[p], earlier.at[p, group], t_send.at[p, g - 1], t_recv.at[p, group],
            device_id=counterpart(g), device_id_type=MESH)

    def d_copy(p, to_odd, to_x):
        return pltpu.make_async_remote_copy(
            dsend.at[p, to_odd, to_x], far.at[p, strip],
            d_send, d_recv.at[p], device_id={"ctx": (2 * group + to_odd) * NX + to_x}, device_id_type=MESH)

    def pair_states(p):
        columns = slice(p * PAIR, (p + 1) * PAIR)
        whole = None
        for c in range(SEG // CHUNK):
            arrived = kv.at[(slice(None), *kv_part(p, c))]
            pltpu.make_async_copy(arrived, arrived, kv_sem.at[p, c]).wait()
            for j in range(c * CHUNK // LEAF, (c + 1) * CHUNK // LEAF):
                rows = slice(j * LEAF, (j + 1) * LEAF)
                both = dot(kv[0, rows, columns], kv[1, rows, columns], TN)
                two = both[:HEAD_DIM, :HEAD_DIM], both[HEAD_DIM:, HEAD_DIM:]
                for i in range(2):
                    leaf_state[j, 2 * p + i] = two[i]
                whole = two if whole is None else [m + n for m, n in zip(whole, two)]
        for i in range(2):
            for r in range(4):
                own[p, 4 * i + r] = whole[i][r * STRIP:(r + 1) * STRIP]
        if p == 0:
            pl.semaphore_wait(barrier, len(AROUND) + NH - 1 + group)
        for dz, dx in AROUND:
            x_copy(p, dz, dx).start()
        pltpu.make_async_copy(own.at[p, strip], xrecv.at[p, odd, x], x_recv.at[p, odd]).start()

    pair_states(0)
    for g in range(GROUPS - 1):
        @pl.when(group > g)
        def _():
            pl.semaphore_signal(ready.at[group - 1], 1, device_id=counterpart(g), device_id_type=MESH)
    q_copy.start()
    pair_states(1)
    for copy in small:
        copy.wait()

    for h in range(HEADS_HERE):
        s = [leaf_state[j, h] for j in range(LEAVES)]
        sums = fenwick(s, weight(h, 1), weight(h, 2), weight(h, 3))
        local[0, h] = jnp.zeros((HEAD_DIM, HEAD_DIM), jnp.bfloat16)
        for j in range(1, LEAVES):
            local[j, h] = sums[j].astype(jnp.bfloat16)

    causal = lax.broadcasted_iota(jnp.int32, (LEAF, LEAF), 1) <= lax.broadcasted_iota(jnp.int32, (LEAF, LEAF), 0)

    def near(j, _):
        rows = pl.ds(pl.multiple_of(j * LEAF, LEAF), LEAF)
        for h in range(HEADS_HERE):
            columns = slice(h * HEAD_DIM, (h + 1) * HEAD_DIM)
            qs = q[rows, columns]
            scores = dot(qs, kv[0, rows, columns], NT)
            rounded = jnp.where(causal, scores * weight(h, 0), 0.0).astype(jnp.bfloat16)
            comb[h, rows] = dot(rounded, kv[1, rows, columns]) + dot(qs, local[j, h])
        return 0

    q_copy.wait()
    lax.fori_loop(0, 3, near, 0)

    pairs = range(HEADS_HERE // 2)

    def weigh(p, i, base):
        h = 2 * p + lax.div(x, 2)
        row = [xrecv[p, i, j] for j in range(NX)]
        if i:
            even = (xrecv[p, 0, 0] + xrecv[p, 0, 1]) + (xrecv[p, 0, 2] + xrecv[p, 0, 3])
            base = base + weight(h, 6) * even
        sums = fenwick(row, weight(h, 4), weight(h, 5))
        dsend[p, i, 0] = base
        for j in range(1, NX):
            dsend[p, i, j] = base + sums[j]

    def give_row(p, i):
        for dx in (2, 1, 3):
            d_copy(p, i, lax.rem(x + dx, NX)).start()
        @pl.when(odd != i)
        def _():
            d_copy(p, i, x).start()

    def give_back(p, i, base):
        weigh(p, i, base)
        give_row(p, i)

    def keep(p):
        pltpu.make_async_copy(dsend.at[p, odd, x], far.at[p, strip], d_recv.at[p]).start()

    def row_arrives(p, i):
        pltpu.make_async_copy(xrecv.at[p, i], xrecv.at[p, i], x_recv.at[p, i]).wait()

    @pl.when(group == 0)
    def _():
        for p in pairs:
            row_arrives(p, 0)
            give_back(p, 0, jnp.zeros((STRIP, HEAD_DIM), jnp.float32))
    for p in pairs:
        @pl.when(group > 0)
        def _():
            row_arrives(p, 0)
        row_arrives(p, 1)
        total[p] = sum(xrecv[p, i, j] for i in range(2) for j in range(NX))
        for g in range(GROUPS - 1, 0, -1):
            @pl.when(group < g)
            def _():
                if p == 0:
                    pl.semaphore_wait(ready.at[g - 1], 1)
                t_copy(p, g).start()

    reached = jnp.where(group == GROUPS - 1, 4, 3)
    lax.fori_loop(3, reached, near, 0)

    for p in pairs:
        for g in range(GROUPS - 1):
            @pl.when(group > g)
            def _():
                pltpu.make_async_copy(earlier.at[p, g], earlier.at[p, g], t_recv.at[p, g]).wait()
        h = 2 * p + lax.div(x, 2)
        far_weight = jnp.where(group >= 2, weight(h, 8), 0.0)
        base = (
            (far_weight + jnp.where(group == 1, weight(h, 7), 0.0)) * earlier[p, 0]
            + far_weight * earlier[p, 1]
            + jnp.where(group == 3, weight(h, 7), 0.0) * earlier[p, 2])
        @pl.when(group == 0)
        def _():
            give_back(p, 1, base)
        @pl.when(group > 0)
        def _():
            weigh(p, 0, base)
            weigh(p, 1, base)
            for dz, dx in AROUND:
                d_copy(p, lax.rem(odd + dz, 2), lax.rem(x + dx, NX)).start()
        keep(p)

    lax.fori_loop(reached, LEAVES, near, 0)

    def s_copy(c, d):
        return pltpu.make_async_remote_copy(
            ssq.at[c], ssq_in.at[c, d - 1], s_send.at[c], s_recv.at[c],
            device_id={"head": lax.rem(head + d, NH)}, device_id_type=MESH)

    ones = jnp.ones((8, 2 * HEAD_DIM), jnp.bfloat16)
    zero = jnp.zeros((HEAD_DIM, HEAD_DIM), jnp.bfloat16)
    for p in pairs:
        pltpu.make_async_copy(far.at[p], far.at[p], d_recv.at[p]).wait()
        first, second = [
            far[p, 4 * i:4 * i + 4].reshape(HEAD_DIM, HEAD_DIM).astype(jnp.bfloat16) for i in range(2)]
        state = jnp.concatenate([
            jnp.concatenate([first, zero], axis=1), jnp.concatenate([zero, second], axis=1)], axis=0)
        for j in range(LEAVES):
            rows = slice(j * LEAF, (j + 1) * LEAF)
            if j % 4 == 0:
                both = dot(q[j * LEAF:(j + 4) * LEAF, p * PAIR:(p + 1) * PAIR], state)
            squares = square_sum[rows] if p else None
            for i in range(2):
                value = comb[2 * p + i, rows] + both[
                    j % 4 * LEAF:(j % 4 + 1) * LEAF, i * HEAD_DIM:(i + 1) * HEAD_DIM]
                comb[2 * p + i, rows] = value
                squares = value * value if squares is None else squares + value * value
            if p == 0:
                square_sum[rows] = squares
                continue
            top = squares.astype(jnp.bfloat16)
            rest = (squares - top.astype(jnp.float32)).astype(jnp.bfloat16)
            line = dot(ones, jnp.concatenate([top, rest], axis=1), NT)
            c, i = divmod(j, LEAVES // CHUNKS)
            ssq[c, 2 * i:2 * i + 1] = line[:1, :HEAD_DIM]
            ssq[c, 2 * i + 1:2 * i + 2] = line[:1, HEAD_DIM:]
            if i == LEAVES // CHUNKS - 1:
                for d in range(1, NH):
                    s_copy(c, d).start()

    for c in range(CHUNKS):
        pltpu.make_async_copy(ssq_in.at[c], ssq_in.at[c], s_recv.at[c]).wait()
        a = [ssq[c]] + [ssq_in[c, d] for d in range(NH - 1)]
        whole = ((a[0] + a[1]) + (a[2] + a[3])) + ((a[4] + a[5]) + (a[6] + a[7]))
        inverse = lax.rsqrt(whole * (1.0 / D) + EPSILON).T
        for i in range(ROWS // HEAD_DIM):
            rows = slice(c * ROWS + i * HEAD_DIM, c * ROWS + (i + 1) * HEAD_DIM)
            for h in range(HEADS_HERE):
                columns = slice(h * HEAD_DIM, (h + 1) * HEAD_DIM)
                out_ref[rows, columns] = (
                    comb[h, rows] * inverse[:, i:i + 1] * gain[:, columns]).astype(jnp.bfloat16)

    for ref, sem in ((own, x_send), (dsend, d_send)):
        sent = ref.reshape(4 * NX, STRIP, HEAD_DIM).at[pl.ds(0, 2 * len(AROUND))]
        pltpu.make_async_copy(sent, sent, sem).wait()
    for p in pairs:
        for g in range(1, GROUPS):
            @pl.when(group < g)
            def _():
                t_copy(p, g).wait_send()
    for c in range(CHUNKS):
        pltpu.make_async_copy(ssq_in.at[c], ssq_in.at[c], s_send.at[c]).wait()


def shards(queries, keys, values, level_table, head_table, gain):
    f32, bf16 = jnp.float32, jnp.bfloat16
    dma = pltpu.SemaphoreType.DMA
    square, strip = (HEAD_DIM, HEAD_DIM), (STRIP, HEAD_DIM)
    anywhere = pl.BlockSpec(memory_space=pltpu.HBM)
    vmem = pl.BlockSpec(memory_space=pltpu.VMEM)
    return pl.pallas_call(
        kernel,
        out_shape=pltpu.VMEM((SEG, WIDTH), bf16),
        in_specs=[anywhere] * 6,
        out_specs=vmem,
        scratch_shapes=[
            pltpu.SMEM(level_table.shape, f32),
            pltpu.SMEM(head_table.shape, jnp.int32),
            pltpu.VMEM((1, WIDTH), f32),
            pltpu.VMEM((SEG, WIDTH), bf16),
            pltpu.VMEM((2, SEG, WIDTH), bf16),
            pltpu.VMEM((HEADS_HERE, SEG, HEAD_DIM), f32),
            pltpu.VMEM((SEG, HEAD_DIM), f32),
            pltpu.VMEM((LEAVES, HEADS_HERE, *square), f32),
            pltpu.VMEM((LEAVES, HEADS_HERE, *square), bf16),
            pltpu.VMEM((2, 8, *strip), f32),
            pltpu.VMEM((2, 2, NX, *strip), f32),
            pltpu.VMEM((2, *strip), f32),
            pltpu.VMEM((2, GROUPS - 1, *strip), f32),
            pltpu.VMEM((2, 2, NX, *strip), f32),
            pltpu.VMEM((2, 8, *strip), f32),
            pltpu.VMEM((CHUNKS, ROWS // HEAD_DIM, HEAD_DIM), f32),
            pltpu.VMEM((CHUNKS, NH - 1, ROWS // HEAD_DIM, HEAD_DIM), f32),
            dma((3,)), dma((HEADS_HERE // 2, SEG // CHUNK)), dma,
            dma, dma((2, 2)),
            dma((2, GROUPS - 1)), dma((2, GROUPS - 1)),
            dma, dma((2,)),
            dma((CHUNKS,)), dma((CHUNKS,)),
            pltpu.SemaphoreType.REGULAR((GROUPS - 1,)),
        ],
        compiler_params=pltpu.CompilerParams(
            collective_id=0, has_side_effects=True, vmem_limit_bytes=40 * 1024 * 1024),
        name="attend",
    )(*[pltpu.with_memory_space_constraint(a, pltpu.HBM) for a in
       (queries, keys, values, level_table, head_table, gain.reshape(1, WIDTH))])


def solution(mesh):
    return jax.shard_map(
        shards,
        mesh=mesh,
        in_specs=(P("ctx", "head"), P("ctx", "head"), P("ctx", "head"), P(), P(), P("head")),
        out_specs=P("ctx", "head"),
        check_vma=False,
    )
```

```python
import functools

import jax
import jax.numpy as jnp
import numpy as np
from jax import lax
from jax.experimental import pallas as pl
from jax.experimental.pallas import tpu as pltpu
from jax.sharding import PartitionSpec as P

HEAD_DIM = 128
LEAF = 256
LEAVES = 8
D = 4096
HEADS_HERE = 4
SEG = LEAF * LEAVES
WIDTH = HEADS_HERE * HEAD_DIM
NX, GROUPS, NH = 4, 4, 8
STRIP = HEAD_DIM // 4
PAIR = 2 * HEAD_DIM
CHUNK = 8 * LEAF
AROUND = [(1, 2), (1, 1), (1, 3), (0, 2), (1, 0), (0, 1), (0, 3)]
CHUNKS = 2
ROWS = SEG // CHUNKS
EPSILON = 1e-06
MESH = pl.DeviceIdType.MESH
SCALES = [float(np.float32(1.0) / np.sqrt(np.float32(LEAF * 2 ** max(l - 1, 0)))) for l in range(9)]

NT = (((1,), (1,)), ((), ()))
TN = (((0,), (0,)), ((), ()))


def dot(a, b, dims=(((1,), (0,)), ((), ()))):
    return lax.dot_general(a, b, dims, preferred_element_type=jnp.float32)


def fenwick(states, one, two, four=None):
    out = []
    pair = states[0] + states[1]
    out.append(None)
    out.append(one * states[0])
    out.append(two * pair)
    out.append(out[2] + one * states[2])
    if four is None:
        return out
    pair_b = states[4] + states[5]
    quad = four * (pair + (states[2] + states[3]))
    out.append(quad)
    out.append(quad + one * states[4])
    out.append(quad + two * pair_b)
    out.append(out[6] + one * states[6])
    return out


def kernel(
    q_hbm, k_hbm, v_hbm, table_hbm, head_table_hbm, gain_hbm, out_ref,
    table, head_table, gain, q, kv, comb, square_sum, leaf_state, local, own, xrecv, total, earlier, dsend, far,
    ssq, ssq_in, small_sem, kv_sem, q_sem, x_send, x_recv, t_send, t_recv, d_send, d_recv, s_send, s_recv, ready,
):
    head = lax.axis_index("head")
    ctx = lax.axis_index("ctx")
    x = lax.rem(ctx, NX)
    z = lax.div(ctx, NX)
    group = lax.div(z, 2)
    odd = lax.rem(z, 2)
    part = lax.rem(odd + lax.div(z, 4), 2)

    def kv_part(p, c):
        return pl.ds(c * CHUNK, CHUNK), pl.ds(p * PAIR, PAIR)

    def kv_start(p):
        for c in range(SEG // CHUNK):
            here = kv_part(p, c)
            pltpu.make_async_copy(k_hbm.at[here], kv.at[(0, *here)], kv_sem.at[p, c]).start()
            pltpu.make_async_copy(v_hbm.at[here], kv.at[(1, *here)], kv_sem.at[p, c]).start()

    def near_by(dz, dx):
        to_odd, to_x = lax.rem(odd + dz, 2), lax.rem(x + dx, NX)
        return to_odd, to_x, {"ctx": (2 * group + to_odd) * NX + to_x}

    def counterpart(g):
        return {"ctx": (2 * g + lax.rem(part + g // 2, 2)) * NX + x}

    barrier = pltpu.get_barrier_semaphore()
    for dz, dx in AROUND:
        pl.semaphore_signal(barrier, 1, device_id=near_by(dz, dx)[2], device_id_type=MESH)
    kv_start(0)
    for d in range(1, NH):
        pl.semaphore_signal(barrier, 1, device_id={"head": lax.rem(head + d, NH)}, device_id_type=MESH)
    for g in range(1, GROUPS):
        @pl.when(group < g)
        def _():
            pl.semaphore_signal(barrier, 1, device_id=counterpart(g), device_id_type=MESH)
    kv_start(1)
    small = [
        pltpu.make_async_copy(a, b, small_sem.at[i])
        for i, (a, b) in enumerate(((table_hbm, table), (head_table_hbm, head_table), (gain_hbm, gain)))]
    for copy in small:
        copy.start()
    q_copy = pltpu.make_async_copy(q_hbm, q, q_sem)
    for g in range(GROUPS - 1):
        for p in range(HEADS_HERE // 2):
            earlier[p, g] = jnp.zeros((STRIP, HEAD_DIM), jnp.float32)

    def weight(h, level):
        return table[head_table[head * HEADS_HERE + h], level] * SCALES[level]

    strip = 2 * x + part

    def x_copy(p, dz, dx):
        to_odd, to_x, to = near_by(dz, dx)
        return pltpu.make_async_remote_copy(
            own.at[p, 2 * to_x + lax.rem(to_odd + lax.div(z, 4), 2)], xrecv.at[p, odd, x],
            x_send, x_recv.at[p, odd], device_id=to, device_id_type=MESH)

    def t_copy(p, g):
        return pltpu.make_async_remote_copy(
            total.at[p], earlier.at[p, group], t_send.at[p, g - 1], t_recv.at[p, group],
            device_id=counterpart(g), device_id_type=MESH)

    def d_copy(p, to_odd, to_x):
        return pltpu.make_async_remote_copy(
            dsend.at[p, to_odd, to_x], far.at[p, strip],
            d_send, d_recv.at[p], device_id={"ctx": (2 * group + to_odd) * NX + to_x}, device_id_type=MESH)

    def pair_states(p):
        columns = slice(p * PAIR, (p + 1) * PAIR)
        whole = None
        for c in range(SEG // CHUNK):
            arrived = kv.at[(slice(None), *kv_part(p, c))]
            pltpu.make_async_copy(arrived, arrived, kv_sem.at[p, c]).wait()
            for j in range(c * CHUNK // LEAF, (c + 1) * CHUNK // LEAF):
                rows = slice(j * LEAF, (j + 1) * LEAF)
                both = dot(kv[0, rows, columns], kv[1, rows, columns], TN)
                two = both[:HEAD_DIM, :HEAD_DIM], both[HEAD_DIM:, HEAD_DIM:]
                for i in range(2):
                    leaf_state[j, 2 * p + i] = two[i]
                whole = two if whole is None else [m + n for m, n in zip(whole, two)]
        for i in range(2):
            for r in range(4):
                own[p, 4 * i + r] = whole[i][r * STRIP:(r + 1) * STRIP]
        if p == 0:
            pl.semaphore_wait(barrier, len(AROUND) + NH - 1 + group)
        for dz, dx in AROUND:
            x_copy(p, dz, dx).start()
        pltpu.make_async_copy(own.at[p, strip], xrecv.at[p, odd, x], x_recv.at[p, odd]).start()

    pair_states(0)
    for g in range(GROUPS - 1):
        @pl.when(group > g)
        def _():
            pl.semaphore_signal(ready.at[group - 1], 1, device_id=counterpart(g), device_id_type=MESH)
    q_copy.start()
    pair_states(1)
    for copy in small:
        copy.wait()
    far_weights = [[weight(2 * p + lax.div(x, 2), level) for level in range(4, 9)] for p in range(HEADS_HERE // 2)]

    for h in range(HEADS_HERE):
        s = [leaf_state[j, h] for j in range(LEAVES)]
        sums = fenwick(s, weight(h, 1), weight(h, 2), weight(h, 3))
        local[0, h] = jnp.zeros((HEAD_DIM, HEAD_DIM), jnp.bfloat16)
        for j in range(1, LEAVES):
            local[j, h] = sums[j].astype(jnp.bfloat16)

    causal = lax.broadcasted_iota(jnp.int32, (LEAF, LEAF), 1) <= lax.broadcasted_iota(jnp.int32, (LEAF, LEAF), 0)

    def near(j, _):
        rows = pl.ds(pl.multiple_of(j * LEAF, LEAF), LEAF)
        for h in range(HEADS_HERE):
            columns = slice(h * HEAD_DIM, (h + 1) * HEAD_DIM)
            qs = q[rows, columns]
            scores = dot(qs, kv[0, rows, columns], NT)
            rounded = jnp.where(causal, scores * weight(h, 0), 0.0).astype(jnp.bfloat16)
            comb[h, rows] = dot(rounded, kv[1, rows, columns]) + dot(qs, local[j, h])
        return 0

    q_copy.wait()
    lax.fori_loop(0, 3, near, 0)

    pairs = range(HEADS_HERE // 2)

    def weigh(p, i, base):
        row = [xrecv[p, i, j] for j in range(NX)]
        if i:
            even = (xrecv[p, 0, 0] + xrecv[p, 0, 1]) + (xrecv[p, 0, 2] + xrecv[p, 0, 3])
            base = base + far_weights[p][2] * even
        sums = fenwick(row, far_weights[p][0], far_weights[p][1])
        dsend[p, i, 0] = base
        for j in range(1, NX):
            dsend[p, i, j] = base + sums[j]

    def give_row(p, i):
        for dx in (2, 1, 3):
            d_copy(p, i, lax.rem(x + dx, NX)).start()
        @pl.when(odd != i)
        def _():
            d_copy(p, i, x).start()

    def give_back(p, i, base):
        weigh(p, i, base)
        give_row(p, i)

    def keep(p):
        pltpu.make_async_copy(dsend.at[p, odd, x], far.at[p, strip], d_recv.at[p]).start()

    def row_arrives(p, i):
        pltpu.make_async_copy(xrecv.at[p, i], xrecv.at[p, i], x_recv.at[p, i]).wait()

    @pl.when(group == 0)
    def _():
        for p in pairs:
            row_arrives(p, 0)
            give_back(p, 0, jnp.zeros((STRIP, HEAD_DIM), jnp.float32))
    for p in pairs:
        @pl.when(group > 0)
        def _():
            row_arrives(p, 0)
        row_arrives(p, 1)
        total[p] = sum(xrecv[p, i, j] for i in range(2) for j in range(NX))
        for g in range(1, GROUPS):
            @pl.when(group < g)
            def _():
                if p == 0:
                    pl.semaphore_wait(ready.at[g - 1], 1)
                t_copy(p, g).start()

    reached = jnp.where(group == GROUPS - 1, 4, 3)
    lax.fori_loop(3, reached, near, 0)

    for p in pairs:
        for g in range(GROUPS - 1):
            @pl.when(group > g)
            def _():
                pltpu.make_async_copy(earlier.at[p, g], earlier.at[p, g], t_recv.at[p, g]).wait()
        far_weight = jnp.where(group >= 2, far_weights[p][4], 0.0)
        base = (
            (far_weight + jnp.where(group == 1, far_weights[p][3], 0.0)) * earlier[p, 0]
            + far_weight * earlier[p, 1]
            + jnp.where(group == 3, far_weights[p][3], 0.0) * earlier[p, 2])
        @pl.when(group == 0)
        def _():
            give_back(p, 1, base)
        @pl.when(group > 0)
        def _():
            weigh(p, 0, base)
            weigh(p, 1, base)
            for dz, dx in AROUND:
                d_copy(p, lax.rem(odd + dz, 2), lax.rem(x + dx, NX)).start()
        keep(p)

    lax.fori_loop(reached, LEAVES, near, 0)

    def s_copy(c, d):
        return pltpu.make_async_remote_copy(
            ssq.at[c], ssq_in.at[c, d - 1], s_send.at[c], s_recv.at[c],
            device_id={"head": lax.rem(head + d, NH)}, device_id_type=MESH)

    ones = jnp.ones((8, 2 * HEAD_DIM), jnp.bfloat16)
    zero = jnp.zeros((HEAD_DIM, HEAD_DIM), jnp.bfloat16)
    for p in pairs:
        pltpu.make_async_copy(far.at[p], far.at[p], d_recv.at[p]).wait()
        first, second = [
            far[p, 4 * i:4 * i + 4].reshape(HEAD_DIM, HEAD_DIM).astype(jnp.bfloat16) for i in range(2)]
        state = jnp.concatenate([
            jnp.concatenate([first, zero], axis=1), jnp.concatenate([zero, second], axis=1)], axis=0)
        for j in range(LEAVES):
            rows = slice(j * LEAF, (j + 1) * LEAF)
            if j % 4 == 0:
                both = dot(q[j * LEAF:(j + 4) * LEAF, p * PAIR:(p + 1) * PAIR], state)
            squares = square_sum[rows] if p else None
            for i in range(2):
                value = comb[2 * p + i, rows] + both[
                    j % 4 * LEAF:(j % 4 + 1) * LEAF, i * HEAD_DIM:(i + 1) * HEAD_DIM]
                comb[2 * p + i, rows] = value
                squares = value * value if squares is None else squares + value * value
            if p == 0:
                square_sum[rows] = squares
                continue
            top = squares.astype(jnp.bfloat16)
            rest = (squares - top.astype(jnp.float32)).astype(jnp.bfloat16)
            line = dot(ones, jnp.concatenate([top, rest], axis=1), NT)
            c, i = divmod(j, LEAVES // CHUNKS)
            ssq[c, 2 * i:2 * i + 1] = line[:1, :HEAD_DIM]
            ssq[c, 2 * i + 1:2 * i + 2] = line[:1, HEAD_DIM:]
            if i == LEAVES // CHUNKS - 1:
                for d in range(1, NH):
                    s_copy(c, d).start()

    for c in range(CHUNKS):
        pltpu.make_async_copy(ssq_in.at[c], ssq_in.at[c], s_recv.at[c]).wait()
        a = [ssq[c]] + [ssq_in[c, d] for d in range(NH - 1)]
        whole = ((a[0] + a[1]) + (a[2] + a[3])) + ((a[4] + a[5]) + (a[6] + a[7]))
        inverse = lax.rsqrt(whole * (1.0 / D) + EPSILON).T
        for i in range(ROWS // HEAD_DIM):
            rows = slice(c * ROWS + i * HEAD_DIM, c * ROWS + (i + 1) * HEAD_DIM)
            for h in range(HEADS_HERE):
                columns = slice(h * HEAD_DIM, (h + 1) * HEAD_DIM)
                out_ref[rows, columns] = (
                    comb[h, rows] * inverse[:, i:i + 1] * gain[:, columns]).astype(jnp.bfloat16)

    for ref, sem in ((own, x_send), (dsend, d_send)):
        sent = ref.reshape(4 * NX, STRIP, HEAD_DIM).at[pl.ds(0, 2 * len(AROUND))]
        pltpu.make_async_copy(sent, sent, sem).wait()
    for p in pairs:
        for g in range(1, GROUPS):
            @pl.when(group < g)
            def _():
                t_copy(p, g).wait_send()
    for c in range(CHUNKS):
        pltpu.make_async_copy(ssq_in.at[c], ssq_in.at[c], s_send.at[c]).wait()


def shards(queries, keys, values, level_table, head_table, gain):
    f32, bf16 = jnp.float32, jnp.bfloat16
    dma = pltpu.SemaphoreType.DMA
    square, strip = (HEAD_DIM, HEAD_DIM), (STRIP, HEAD_DIM)
    anywhere = pl.BlockSpec(memory_space=pltpu.HBM)
    vmem = pl.BlockSpec(memory_space=pltpu.VMEM)
    return pl.pallas_call(
        kernel,
        out_shape=pltpu.VMEM((SEG, WIDTH), bf16),
        in_specs=[anywhere] * 6,
        out_specs=vmem,
        scratch_shapes=[
            pltpu.SMEM(level_table.shape, f32),
            pltpu.SMEM(head_table.shape, jnp.int32),
            pltpu.VMEM((1, WIDTH), f32),
            pltpu.VMEM((SEG, WIDTH), bf16),
            pltpu.VMEM((2, SEG, WIDTH), bf16),
            pltpu.VMEM((HEADS_HERE, SEG, HEAD_DIM), f32),
            pltpu.VMEM((SEG, HEAD_DIM), f32),
            pltpu.VMEM((LEAVES, HEADS_HERE, *square), f32),
            pltpu.VMEM((LEAVES, HEADS_HERE, *square), bf16),
            pltpu.VMEM((2, 8, *strip), f32),
            pltpu.VMEM((2, 2, NX, *strip), f32),
            pltpu.VMEM((2, *strip), f32),
            pltpu.VMEM((2, GROUPS - 1, *strip), f32),
            pltpu.VMEM((2, 2, NX, *strip), f32),
            pltpu.VMEM((2, 8, *strip), f32),
            pltpu.VMEM((CHUNKS, ROWS // HEAD_DIM, HEAD_DIM), f32),
            pltpu.VMEM((CHUNKS, NH - 1, ROWS // HEAD_DIM, HEAD_DIM), f32),
            dma((3,)), dma((HEADS_HERE // 2, SEG // CHUNK)), dma,
            dma, dma((2, 2)),
            dma((2, GROUPS - 1)), dma((2, GROUPS - 1)),
            dma, dma((2,)),
            dma((CHUNKS,)), dma((CHUNKS,)),
            pltpu.SemaphoreType.REGULAR((GROUPS - 1,)),
        ],
        compiler_params=pltpu.CompilerParams(
            collective_id=0, has_side_effects=True, vmem_limit_bytes=40 * 1024 * 1024),
        name="attend",
    )(*[pltpu.with_memory_space_constraint(a, pltpu.HBM) for a in
       (queries, keys, values, level_table, head_table, gain.reshape(1, WIDTH))])


def solution(mesh):
    return jax.shard_map(
        shards,
        mesh=mesh,
        in_specs=(P("ctx", "head"), P("ctx", "head"), P("ctx", "head"), P(), P(), P("head")),
        out_specs=P("ctx", "head"),
        check_vma=False,
    )
```

```python
import functools

import jax
import jax.numpy as jnp
import numpy as np
from jax import lax
from jax.experimental import pallas as pl
from jax.experimental.pallas import tpu as pltpu
from jax.sharding import PartitionSpec as P

HEAD_DIM = 128
LEAF = 256
LEAVES = 8
D = 4096
HEADS_HERE = 4
SEG = LEAF * LEAVES
WIDTH = HEADS_HERE * HEAD_DIM
NX, GROUPS, NH = 4, 4, 8
STRIP = HEAD_DIM // 4
PAIR = 2 * HEAD_DIM
CHUNK = 8 * LEAF
AROUND = [(1, 2), (1, 1), (1, 3), (0, 2), (1, 0), (0, 1), (0, 3)]
CHUNKS = 2
ROWS = SEG // CHUNKS
EPSILON = 1e-06
MESH = pl.DeviceIdType.MESH
SCALES = [float(np.float32(1.0) / np.sqrt(np.float32(LEAF * 2 ** max(l - 1, 0)))) for l in range(9)]

NT = (((1,), (1,)), ((), ()))
TN = (((0,), (0,)), ((), ()))


def dot(a, b, dims=(((1,), (0,)), ((), ()))):
    return lax.dot_general(a, b, dims, preferred_element_type=jnp.float32)


def fenwick(states, one, two, four=None):
    out = []
    pair = states[0] + states[1]
    out.append(None)
    out.append(one * states[0])
    out.append(two * pair)
    out.append(out[2] + one * states[2])
    if four is None:
        return out
    pair_b = states[4] + states[5]
    quad = four * (pair + (states[2] + states[3]))
    out.append(quad)
    out.append(quad + one * states[4])
    out.append(quad + two * pair_b)
    out.append(out[6] + one * states[6])
    return out


def kernel(
    q_hbm, k_hbm, v_hbm, table_hbm, head_table_hbm, gain_hbm, out_ref,
    table, head_table, gain, q, kv, comb, square_sum, leaf_state, local, own, xrecv, total, earlier, dsend, far,
    ssq, ssq_in, small_sem, kv_sem, q_sem, x_send, x_recv, t_send, t_recv, d_send, d_recv, s_send, s_recv, ready,
):
    head = lax.axis_index("head")
    ctx = lax.axis_index("ctx")
    x = lax.rem(ctx, NX)
    z = lax.div(ctx, NX)
    group = lax.div(z, 2)
    odd = lax.rem(z, 2)
    part = lax.rem(odd + lax.div(z, 4), 2)

    def kv_part(p, c):
        return pl.ds(c * CHUNK, CHUNK), pl.ds(p * PAIR, PAIR)

    def kv_start(p):
        for c in range(SEG // CHUNK):
            here = kv_part(p, c)
            pltpu.make_async_copy(k_hbm.at[here], kv.at[(0, *here)], kv_sem.at[p, c]).start()
            pltpu.make_async_copy(v_hbm.at[here], kv.at[(1, *here)], kv_sem.at[p, c]).start()

    def near_by(dz, dx):
        to_odd, to_x = lax.rem(odd + dz, 2), lax.rem(x + dx, NX)
        return to_odd, to_x, {"ctx": (2 * group + to_odd) * NX + to_x}

    def counterpart(g):
        return {"ctx": (2 * g + lax.rem(part + g // 2, 2)) * NX + x}

    barrier = pltpu.get_barrier_semaphore()
    for dz, dx in AROUND:
        pl.semaphore_signal(barrier, 1, device_id=near_by(dz, dx)[2], device_id_type=MESH)
    kv_start(0)
    for d in range(1, NH):
        pl.semaphore_signal(barrier, 1, device_id={"head": lax.rem(head + d, NH)}, device_id_type=MESH)
    for g in range(1, GROUPS):
        @pl.when(group < g)
        def _():
            pl.semaphore_signal(barrier, 1, device_id=counterpart(g), device_id_type=MESH)
    kv_start(1)
    small = [
        pltpu.make_async_copy(a, b, small_sem.at[i])
        for i, (a, b) in enumerate(((table_hbm, table), (head_table_hbm, head_table), (gain_hbm, gain)))]
    for copy in small:
        copy.start()
    q_copy = pltpu.make_async_copy(q_hbm, q, q_sem)
    for g in range(GROUPS - 1):
        for p in range(HEADS_HERE // 2):
            earlier[p, g] = jnp.zeros((STRIP, HEAD_DIM), jnp.float32)

    def weight(h, level):
        return table[head_table[head * HEADS_HERE + h], level] * SCALES[level]

    strip = 2 * x + part

    def x_copy(p, dz, dx):
        to_odd, to_x, to = near_by(dz, dx)
        return pltpu.make_async_remote_copy(
            own.at[p, 2 * to_x + lax.rem(to_odd + lax.div(z, 4), 2)], xrecv.at[p, odd, x],
            x_send, x_recv.at[p, odd], device_id=to, device_id_type=MESH)

    def t_copy(p, g):
        return pltpu.make_async_remote_copy(
            total.at[p], earlier.at[p, group], t_send.at[p, g - 1], t_recv.at[p, group],
            device_id=counterpart(g), device_id_type=MESH)

    def d_copy(p, to_odd, to_x):
        return pltpu.make_async_remote_copy(
            dsend.at[p, to_odd, to_x], far.at[p, strip],
            d_send, d_recv.at[p], device_id={"ctx": (2 * group + to_odd) * NX + to_x}, device_id_type=MESH)

    def pair_states(p):
        columns = slice(p * PAIR, (p + 1) * PAIR)
        whole = None
        for c in range(SEG // CHUNK):
            arrived = kv.at[(slice(None), *kv_part(p, c))]
            pltpu.make_async_copy(arrived, arrived, kv_sem.at[p, c]).wait()
            for j in range(c * CHUNK // LEAF, (c + 1) * CHUNK // LEAF):
                rows = slice(j * LEAF, (j + 1) * LEAF)
                both = dot(kv[0, rows, columns], kv[1, rows, columns], TN)
                two = both[:HEAD_DIM, :HEAD_DIM], both[HEAD_DIM:, HEAD_DIM:]
                for i in range(2):
                    leaf_state[j, 2 * p + i] = two[i]
                whole = two if whole is None else [m + n for m, n in zip(whole, two)]
        for i in range(2):
            for r in range(4):
                own[p, 4 * i + r] = whole[i][r * STRIP:(r + 1) * STRIP]
        if p == 0:
            pl.semaphore_wait(barrier, len(AROUND) + NH - 1 + group)
        for dz, dx in AROUND:
            x_copy(p, dz, dx).start()
        pltpu.make_async_copy(own.at[p, strip], xrecv.at[p, odd, x], x_recv.at[p, odd]).start()

    pair_states(0)
    for g in range(GROUPS - 1):
        @pl.when(group > g)
        def _():
            pl.semaphore_signal(ready.at[group - 1], 1, device_id=counterpart(g), device_id_type=MESH)
    q_copy.start()
    pair_states(1)
    for copy in small:
        copy.wait()
    far_weights = [[weight(2 * p + lax.div(x, 2), level) for level in range(4, 9)] for p in range(HEADS_HERE // 2)]

    for h in range(HEADS_HERE):
        s = [leaf_state[j, h] for j in range(LEAVES)]
        sums = fenwick(s, weight(h, 1), weight(h, 2), weight(h, 3))
        local[0, h] = jnp.zeros((HEAD_DIM, HEAD_DIM), jnp.bfloat16)
        for j in range(1, LEAVES):
            local[j, h] = sums[j].astype(jnp.bfloat16)

    causal = lax.broadcasted_iota(jnp.int32, (LEAF, LEAF), 1) <= lax.broadcasted_iota(jnp.int32, (LEAF, LEAF), 0)

    def near(j, _):
        rows = pl.ds(pl.multiple_of(j * LEAF, LEAF), LEAF)
        for h in range(HEADS_HERE):
            columns = slice(h * HEAD_DIM, (h + 1) * HEAD_DIM)
            qs = q[rows, columns]
            scores = dot(qs, kv[0, rows, columns], NT)
            rounded = jnp.where(causal, scores * weight(h, 0), 0.0).astype(jnp.bfloat16)
            comb[h, rows] = dot(rounded, kv[1, rows, columns]) + dot(qs, local[j, h])
        return 0

    q_copy.wait()
    lax.fori_loop(0, 3, near, 0)

    pairs = range(HEADS_HERE // 2)

    def weigh(p, i, base):
        row = [xrecv[p, i, j] for j in range(NX)]
        if i:
            even = (xrecv[p, 0, 0] + xrecv[p, 0, 1]) + (xrecv[p, 0, 2] + xrecv[p, 0, 3])
            base = base + far_weights[p][2] * even
        sums = fenwick(row, far_weights[p][0], far_weights[p][1])
        dsend[p, i, 0] = base
        for j in range(1, NX):
            dsend[p, i, j] = base + sums[j]

    def give_row(p, i):
        for dx in (2, 1, 3):
            d_copy(p, i, lax.rem(x + dx, NX)).start()
        @pl.when(odd != i)
        def _():
            d_copy(p, i, x).start()

    def give_back(p, i, base):
        weigh(p, i, base)
        give_row(p, i)

    def keep(p):
        pltpu.make_async_copy(dsend.at[p, odd, x], far.at[p, strip], d_recv.at[p]).start()

    def row_arrives(p, i):
        pltpu.make_async_copy(xrecv.at[p, i], xrecv.at[p, i], x_recv.at[p, i]).wait()

    @pl.when(group == 0)
    def _():
        for p in pairs:
            row_arrives(p, 0)
            give_back(p, 0, jnp.zeros((STRIP, HEAD_DIM), jnp.float32))
    for p in pairs:
        @pl.when(group > 0)
        def _():
            row_arrives(p, 0)
        row_arrives(p, 1)
        total[p] = sum(xrecv[p, i, j] for i in range(2) for j in range(NX))
        for g in range(1, GROUPS):
            @pl.when(group < g)
            def _():
                if p == 0:
                    pl.semaphore_wait(ready.at[g - 1], 1)
                t_copy(p, g).start()

    @pl.when(group > 0)
    def _():
        for p in pairs:
            for i in range(2):
                weigh(p, i, jnp.zeros((STRIP, HEAD_DIM), jnp.float32))

    reached = jnp.where(group == GROUPS - 1, 4, 3)
    lax.fori_loop(3, reached, near, 0)

    for p in pairs:
        for g in range(GROUPS - 1):
            @pl.when(group > g)
            def _():
                pltpu.make_async_copy(earlier.at[p, g], earlier.at[p, g], t_recv.at[p, g]).wait()
        far_weight = jnp.where(group >= 2, far_weights[p][4], 0.0)
        base = (
            (far_weight + jnp.where(group == 1, far_weights[p][3], 0.0)) * earlier[p, 0]
            + far_weight * earlier[p, 1]
            + jnp.where(group == 3, far_weights[p][3], 0.0) * earlier[p, 2])
        @pl.when(group == 0)
        def _():
            give_back(p, 1, base)
        @pl.when(group > 0)
        def _():
            dsend[p] = dsend[p] + base
            for dz, dx in AROUND:
                d_copy(p, lax.rem(odd + dz, 2), lax.rem(x + dx, NX)).start()
        keep(p)

    lax.fori_loop(reached, LEAVES, near, 0)

    def s_copy(c, d):
        return pltpu.make_async_remote_copy(
            ssq.at[c], ssq_in.at[c, d - 1], s_send.at[c], s_recv.at[c],
            device_id={"head": lax.rem(head + d, NH)}, device_id_type=MESH)

    ones = jnp.ones((8, 2 * HEAD_DIM), jnp.bfloat16)
    zero = jnp.zeros((HEAD_DIM, HEAD_DIM), jnp.bfloat16)
    for p in pairs:
        pltpu.make_async_copy(far.at[p], far.at[p], d_recv.at[p]).wait()
        first, second = [
            far[p, 4 * i:4 * i + 4].reshape(HEAD_DIM, HEAD_DIM).astype(jnp.bfloat16) for i in range(2)]
        state = jnp.concatenate([
            jnp.concatenate([first, zero], axis=1), jnp.concatenate([zero, second], axis=1)], axis=0)
        for j in range(LEAVES):
            rows = slice(j * LEAF, (j + 1) * LEAF)
            if j % 4 == 0:
                both = dot(q[j * LEAF:(j + 4) * LEAF, p * PAIR:(p + 1) * PAIR], state)
            squares = square_sum[rows] if p else None
            for i in range(2):
                value = comb[2 * p + i, rows] + both[
                    j % 4 * LEAF:(j % 4 + 1) * LEAF, i * HEAD_DIM:(i + 1) * HEAD_DIM]
                comb[2 * p + i, rows] = value
                squares = value * value if squares is None else squares + value * value
            if p == 0:
                square_sum[rows] = squares
                continue
            top = squares.astype(jnp.bfloat16)
            rest = (squares - top.astype(jnp.float32)).astype(jnp.bfloat16)
            line = dot(ones, jnp.concatenate([top, rest], axis=1), NT)
            c, i = divmod(j, LEAVES // CHUNKS)
            ssq[c, 2 * i:2 * i + 1] = line[:1, :HEAD_DIM]
            ssq[c, 2 * i + 1:2 * i + 2] = line[:1, HEAD_DIM:]
            if i == LEAVES // CHUNKS - 1:
                for d in range(1, NH):
                    s_copy(c, d).start()

    for c in range(CHUNKS):
        pltpu.make_async_copy(ssq_in.at[c], ssq_in.at[c], s_recv.at[c]).wait()
        a = [ssq[c]] + [ssq_in[c, d] for d in range(NH - 1)]
        whole = ((a[0] + a[1]) + (a[2] + a[3])) + ((a[4] + a[5]) + (a[6] + a[7]))
        inverse = lax.rsqrt(whole * (1.0 / D) + EPSILON).T
        for i in range(ROWS // HEAD_DIM):
            rows = slice(c * ROWS + i * HEAD_DIM, c * ROWS + (i + 1) * HEAD_DIM)
            for h in range(HEADS_HERE):
                columns = slice(h * HEAD_DIM, (h + 1) * HEAD_DIM)
                out_ref[rows, columns] = (
                    comb[h, rows] * inverse[:, i:i + 1] * gain[:, columns]).astype(jnp.bfloat16)

    for ref, sem in ((own, x_send), (dsend, d_send)):
        sent = ref.reshape(4 * NX, STRIP, HEAD_DIM).at[pl.ds(0, 2 * len(AROUND))]
        pltpu.make_async_copy(sent, sent, sem).wait()
    for p in pairs:
        for g in range(1, GROUPS):
            @pl.when(group < g)
            def _():
                t_copy(p, g).wait_send()
    for c in range(CHUNKS):
        pltpu.make_async_copy(ssq_in.at[c], ssq_in.at[c], s_send.at[c]).wait()


def shards(queries, keys, values, level_table, head_table, gain):
    f32, bf16 = jnp.float32, jnp.bfloat16
    dma = pltpu.SemaphoreType.DMA
    square, strip = (HEAD_DIM, HEAD_DIM), (STRIP, HEAD_DIM)
    anywhere = pl.BlockSpec(memory_space=pltpu.HBM)
    vmem = pl.BlockSpec(memory_space=pltpu.VMEM)
    return pl.pallas_call(
        kernel,
        out_shape=pltpu.VMEM((SEG, WIDTH), bf16),
        in_specs=[anywhere] * 6,
        out_specs=vmem,
        scratch_shapes=[
            pltpu.SMEM(level_table.shape, f32),
            pltpu.SMEM(head_table.shape, jnp.int32),
            pltpu.VMEM((1, WIDTH), f32),
            pltpu.VMEM((SEG, WIDTH), bf16),
            pltpu.VMEM((2, SEG, WIDTH), bf16),
            pltpu.VMEM((HEADS_HERE, SEG, HEAD_DIM), f32),
            pltpu.VMEM((SEG, HEAD_DIM), f32),
            pltpu.VMEM((LEAVES, HEADS_HERE, *square), f32),
            pltpu.VMEM((LEAVES, HEADS_HERE, *square), bf16),
            pltpu.VMEM((2, 8, *strip), f32),
            pltpu.VMEM((2, 2, NX, *strip), f32),
            pltpu.VMEM((2, *strip), f32),
            pltpu.VMEM((2, GROUPS - 1, *strip), f32),
            pltpu.VMEM((2, 2, NX, *strip), f32),
            pltpu.VMEM((2, 8, *strip), f32),
            pltpu.VMEM((CHUNKS, ROWS // HEAD_DIM, HEAD_DIM), f32),
            pltpu.VMEM((CHUNKS, NH - 1, ROWS // HEAD_DIM, HEAD_DIM), f32),
            dma((3,)), dma((HEADS_HERE // 2, SEG // CHUNK)), dma,
            dma, dma((2, 2)),
            dma((2, GROUPS - 1)), dma((2, GROUPS - 1)),
            dma, dma((2,)),
            dma((CHUNKS,)), dma((CHUNKS,)),
            pltpu.SemaphoreType.REGULAR((GROUPS - 1,)),
        ],
        compiler_params=pltpu.CompilerParams(
            collective_id=0, has_side_effects=True, vmem_limit_bytes=40 * 1024 * 1024),
        name="attend",
    )(*[pltpu.with_memory_space_constraint(a, pltpu.HBM) for a in
       (queries, keys, values, level_table, head_table, gain.reshape(1, WIDTH))])


def solution(mesh):
    return jax.shard_map(
        shards,
        mesh=mesh,
        in_specs=(P("ctx", "head"), P("ctx", "head"), P("ctx", "head"), P(), P(), P("head")),
        out_specs=P("ctx", "head"),
        check_vma=False,
    )
```
